128 devices in a mesh: fsdp: 4 (over z_hi, core), vocab: 32 (over y, x, z_lo).
Axes of the slice: x: 4, y: 4, z: 4 (z_hi: 2, z_lo: 2; z = z_hi * 2 + z_lo), core: 2. Of those that a mesh axis runs over, the one named last changes fastest.
Arguments:
- head_table: bfloat16 [81920, 7168], P('vocab', 'fsdp'), may hold values from -32 to 32
- embed_table: bfloat16 [81920, 7168], P('vocab', 'fsdp'), may hold values from -6 to 6
- hidden: bfloat16 [4, 256, 7168], P(None, ('fsdp', 'vocab')), may hold values from -128 to 128
- norm_gain: float32 [7168], replicated, may hold values from 0.5 to 1.5
- tokens: int32 [4, 256], P(None, 'fsdp'), may hold values from 0 to 81919
Outputs:
- logprobs: float32 [4, 256], P(None, 'fsdp')
- embeddings: bfloat16 [4, 256, 7168], P(None, 'vocab', 'fsdp')
The draws below stay inside these ranges and needn't reach their ends.
All inputs are finite; a program needn't handle non-finite values.
Results may differ from the reference program's by a relative error of at most 0.0055.
Values may be sent and summed in bfloat16 or wider, within the bound.
A program may use at most 256 MiB of HBM per device.

```python
import math
import jax
import jax.numpy as jnp
from jax import lax

V = 81920
D = 7168
QB = 128
STEPS = 4
ROWS = 256
N_VOCAB = 32


def draw_hidden(key, part):
    key = jax.random.fold_in(key, 11)
    row_key, column_key, noise_key = jax.random.split(key, 3)
    row_scale = jnp.exp(jax.random.uniform(row_key, (STEPS, ROWS, 1), jnp.float32, 0.0, math.log(10.0)))
    column_scale = jnp.exp(jax.random.uniform(column_key, (1, 1, D), jnp.float32, 0.0, math.log(3.0)))
    noise = jax.random.truncated_normal(noise_key, -4.0, 4.0, (STEPS, ROWS, D), jnp.float32)
    values = noise * row_scale * column_scale
    return values.astype(jnp.bfloat16)


def draw_head_table(key, part):
    key = jax.random.fold_in(key, 23)
    spread = 3.0 / math.sqrt(D)
    weights = jax.random.truncated_normal(key, -4.0, 4.0, (V, D), jnp.float32) * spread
    return weights.astype(jnp.bfloat16)


def draw_tokens(key, part):
    key = jax.random.fold_in(key, 37)
    place_key, crowd_key, near_key, even_key, end_key = jax.random.split(key, 5)
    span_width = V // 64
    region_start = jax.random.randint(place_key, (STEPS, 1), 0, 64) * span_width
    crowded = jax.random.randint(crowd_key, (STEPS, ROWS), 0, 2) == 1
    nearby = region_start + jax.random.randint(near_key, (STEPS, ROWS), 0, span_width)
    anywhere = jax.random.randint(even_key, (STEPS, ROWS), 0, V)
    chosen = jnp.where(crowded, nearby, anywhere).astype(jnp.int32)
    end_rows = jax.random.permutation(end_key, ROWS)[:2]
    chosen = chosen.at[0, end_rows[0]].set(V - 1)
    chosen = chosen.at[0, end_rows[1]].set(0)
    return chosen


def level_of(rng, extent, shards, low, high):
    def one(dim, shards_of):
        heights = jax.random.uniform(jax.random.fold_in(jax.random.fold_in(rng, 6), dim), (shards_of,), jnp.float32, low / len(shards), high / len(shards))
        return jnp.repeat(jnp.exp(heights), extent[dim] // shards_of).reshape((-1,) + (1,) * (len(extent) - dim - 1))

    factor_of = one(*shards[0])
    for cut in shards[1:]:
        factor_of = factor_of * one(*cut)
    return factor_of


def gaussian(own_key, dims, scale, reach, cuts=(), dtype=jnp.bfloat16):
    factor_of = level_of(own_key, dims, cuts, -0.22, 0.18) if cuts else 1.0
    entries = jax.random.normal(own_key, dims, jnp.float32) * scale * factor_of
    return jnp.minimum(jnp.maximum(entries, -reach), reach).astype(dtype)


def setup_inputs(seed: int = 0) -> dict:
    arg_keys = jax.random.split(jax.random.key(seed), 6)
    return {
        "head_table": draw_head_table(jax.random.fold_in(arg_keys[5], 71), 0),
        "embed_table": gaussian(arg_keys[1], (V, D), 1.0, 6.0, ((0, 32), (1, 4))),
        "hidden": draw_hidden(jax.random.fold_in(arg_keys[5], 71), 0),
        "norm_gain": jnp.clip(1.0 + 0.1 * jax.random.normal(arg_keys[3], (D,), jnp.float32), 0.5, 1.5),
        "tokens": draw_tokens(jax.random.fold_in(arg_keys[5], 71), 0),
    }


def dequantize(weights):
    height, width = weights.shape
    blocks = weights.astype(jnp.float32).reshape(height // QB, QB, width // QB, QB)
    largest = lax.optimization_barrier(jnp.max(jnp.abs(blocks), axis=(1, 3), keepdims=True))
    scales = (largest + 1e-06) / 7.0
    coded = jnp.floor(blocks / scales + 0.5)
    return (coded * scales).astype(jnp.bfloat16).reshape(height, width)

def normalize(hidden, norm_gain):
    values = hidden.astype(jnp.float32)
    mean_square = lax.optimization_barrier(jnp.mean(values * values, axis=-1, keepdims=True))
    return (values * lax.rsqrt(mean_square + 1e-06) * norm_gain).astype(jnp.bfloat16)

def reference(head_table, embed_table, hidden, norm_gain, tokens):
    restored = lax.map(dequantize, head_table.reshape(N_VOCAB, V // N_VOCAB, D)).reshape(V, D)
    normed = normalize(hidden, norm_gain)

    def one_step(carry, inputs):
        normed_rows, step_tokens = inputs
        logits = lax.dot_general(normed_rows, restored, (((1,), (1,)), ((), ())), preferred_element_type=jnp.float32)
        maxima = lax.optimization_barrier(jnp.max(logits, axis=1))
        totals = lax.optimization_barrier(jnp.sum(jnp.exp(logits - maxima[:, None]), axis=1))
        targets = jnp.take_along_axis(logits, step_tokens[:, None].astype(jnp.int32), axis=1)[:, 0]
        return (carry, targets - maxima - jnp.log(totals))
    _, logprobs = lax.scan(one_step, jnp.zeros((), jnp.int32), (normed, tokens))
    embeddings = jnp.take(embed_table, tokens, axis=0)
    return (logprobs, embeddings)
```

```python
import jax
import jax.numpy as jnp
from jax import lax
from jax.experimental import pallas as pl
from jax.experimental.pallas import tpu as pltpu
from jax.sharding import PartitionSpec as P

MESH = pl.DeviceIdType.MESH
QB = 128
f32, bf16, i32 = jnp.float32, jnp.bfloat16, jnp.int32
VOC = 2560
WID = 1792
HALF = WID // 2
D = 7168
MT = 640
HM = VOC // 2 // MT


def remote(src, dst, send_sem, recv_sem, device):
    return pltpu.make_async_remote_copy(
        src_ref=src, dst_ref=dst, send_sem=send_sem, recv_sem=recv_sem, device_id=device, device_id_type=MESH
    )


def kernel(
    h_ref, g_ref, t_ref, w_hbm, e_hbm, logp_ref, emb_ref,
    W, EM, OH, US, UR, TOK, X, PS, PR, ZS, ZR, OWN, PK, RA0, RA1, RB, RC, RD, SD, ST,
    w_sem, e_sem, us_s, us_r, tk_s, tk_r, p1_s, p1_r, p2_s, p2_r, p3_s, p3_r,
    co_s, co_r, z_s, z_r, a_s, a_r, b_s, b_r, c_s, c_r, d_s, d_r, st_s, st_r,
):
    fs, vo = lax.axis_index("fsdp"), lax.axis_index("vocab")
    zh, c = fs // 2, fs % 2
    y, x, zl = vo // 8, (vo // 2) % 4, vo % 2
    z = zh * 2 + zl

    def dev(x_, y_, z_, c_):
        x_, y_, z_, c_ = (x_ + 4) % 4, (y_ + 4) % 4, (z_ + 4) % 4, (c_ + 2) % 2
        return ((z_ // 2) * 2 + c_, (y_ * 4 + x_) * 2 + z_ % 2)

    xs = [(x + d) % 4 for d in range(4)]
    ys = [(y + d) % 4 for d in range(4)]
    column = [(i // 2, i % 2) for i in range(8)]
    ring = (1, 3, 2)
    sends = []

    def go(cp):
        cp.start()
        sends.append(cp)

    w_parts, e_parts = 4, 2
    w_cps = [
        pltpu.make_async_copy(w_hbm.at[pl.ds(i * 640, 640)], W.at[pl.ds(i * 640, 640)], w_sem.at[i])
        for i in range(w_parts)
    ]
    e_cps = [
        pltpu.make_async_copy(e_hbm.at[pl.ds(i * 1280, 1280)], EM.at[pl.ds(i * 1280, 1280)], e_sem.at[i])
        for i in range(e_parts)
    ]
    for cp in w_cps:
        cp.start()
    for cp in e_cps:
        cp.start()

    barrier = pltpu.get_barrier_semaphore()
    peers = [dev(x, y, z + dz, c + dc) for dz, dc in column[1:]]
    peers += [dev(x + d, y, z, c) for d in ring] + [dev(x, y + d, z, c) for d in ring]
    for peer in peers:
        pl.semaphore_signal(barrier, inc=1, device_id=peer, device_id_type=MESH)

    h = jnp.concatenate([h_ref[s].astype(f32) for s in range(4)], axis=0)
    ms = jnp.sum(h * h, axis=1, keepdims=True) * (1.0 / D)
    normed = h * lax.rsqrt(ms + 1e-06) * g_ref[...]
    for q in range(4):
        lo = normed[:, q * WID : q * WID + HALF]
        hi = normed[:, q * WID + HALF : (q + 1) * WID]
        US[q] = jnp.concatenate([lo, hi], axis=0).astype(bf16)
    UR[0] = US[fs]
    TOK[0] = t_ref[...]
    pl.semaphore_wait(barrier, len(peers))

    unit_cps = []
    for i, (dz, dc) in enumerate(column):
        if i == 0:
            continue
        z2, c2 = (z + dz) % 4, (c + dc) % 2
        cp = remote(US.at[(z2 // 2) * 2 + c2], UR.at[i], us_s.at[i], us_r.at[i], dev(x, y, z2, c2))
        go(cp)
        unit_cps.append(cp)
    tok_cps = []
    for i, (dzh, dc) in enumerate(((0, 0), (0, 1), (1, 0), (1, 1))):
        if i == 0:
            continue
        cp = remote(TOK.at[0], TOK.at[i], tk_s.at[i], tk_r.at[i], dev(x, y, z + 2 * dzh, c + dc))
        go(cp)
        tok_cps.append(cp)

    def restore(part):
        w_cps[part].wait()

        def group(n, _):
            rows = pl.ds(pl.multiple_of(part * 640 + n * QB, QB), QB)
            for j in range(WID // QB):
                block = W[rows, j * QB : (j + 1) * QB].astype(f32)
                scale = (jnp.max(jnp.abs(block), axis=(0, 1), keepdims=True) + 1e-06) / 7.0
                coded = jnp.floor(block / scale + 0.5)
                W[rows, j * QB : (j + 1) * QB] = (coded * scale).astype(bf16)
            return 0

        lax.fori_loop(0, 5, group, 0)

    zs = [(1 - zh) * 2, (1 - zh) * 2 + 1, zh * 2, zh * 2 + 1]

    def units():
        for cp in unit_cps:
            cp.wait_recv()
        for k in range(4):
            dz = (z - zs[k] + 4) % 4
            u0 = UR[dz * 2 + c].astype(f32)
            u1 = UR[dz * 2 + (1 - c)].astype(f32)
            X[k, 0, y, x] = jnp.concatenate([u0[:8], u1[:8]], axis=0).astype(bf16)
            X[k, 1, y, x] = jnp.concatenate([u0[8:], u1[8:]], axis=0).astype(bf16)

    def p1_copy(k, n, j, px, py):
        slot = X.at[k, n, py, px]
        target = dev(x + ring[j], y, z, c) if n == 0 else dev(x, y + ring[j], z, c)
        return remote(slot, slot, p1_s.at[k, n, j], p1_r.at[k, n, j], target)

    def p1_send(k):
        for n in range(2):
            for j in range(3):
                go(p1_copy(k, n, j, x, y))

    def p1_wait(k):
        for j in range(3):
            p1_copy(k, 0, j, xs[4 - ring[j]], y).wait_recv()
            p1_copy(k, 1, j, x, ys[4 - ring[j]]).wait_recv()

    def p2_copy(k, n, j, at):
        slot = X.at[k, 0, at] if n == 0 else X.at[k, 1, :, at]
        step = 1 if j == 0 else 3
        target = dev(x, y + step, z, c) if n == 0 else dev(x + step, y, z, c)
        return remote(slot, slot, p2_s.at[k, n, j], p2_r.at[k, n, j], target)

    def p2_send(k):
        for n in range(2):
            for j in range(2):
                go(p2_copy(k, n, j, y if n == 0 else x))

    def p3_copy(k, n, j, at):
        part = pl.ds(0, 2) if j == 0 else pl.ds(2, 2)
        slot = X.at[k, 0, at, part] if n == 0 else X.at[k, 1, part, at]
        step = 1 if j == 0 else 3
        target = dev(x, y + step, z, c) if n == 0 else dev(x + step, y, z, c)
        return remote(slot, slot, p3_s.at[k, n, j], p3_r.at[k, n, j], target)

    def p3_send(k):
        for j in range(2):
            for n in range(2):
                came = (ys if n == 0 else xs)[3 if j == 0 else 1]
                p2_copy(k, n, j, came).wait_recv()
                go(p3_copy(k, n, j, came))

    def p3_wait(k):
        for j in range(2):
            p3_copy(k, 0, j, ys[2]).wait_recv()
            p3_copy(k, 1, j, xs[2]).wait_recv()

    def logits_tile(k, row):
        rhs = jnp.concatenate([X[k, 0].reshape(256, HALF), X[k, 1].reshape(256, HALF)], axis=1)
        rows = pl.ds(pl.multiple_of(row, MT), MT)
        return lax.dot_general(W[rows, :], rhs, (((1,), (1,)), ((), ())), preferred_element_type=f32)

    def core_copy(k, m):
        return remote(PS.at[k, m], PR.at[k, m], co_s.at[k, m], co_r.at[k, m], dev(x, y, z, c + 1))

    def z_copy(k, m):
        return remote(ZS.at[k, m], ZR.at[k, m], z_s.at[k, m], z_r.at[k, m], dev(x, y, z + 2, c))

    def chunk(k):
        def other(m, _):
            PS[k, m] = logits_tile(k, (1 - c) * (HM * MT) + m * MT).astype(bf16)
            core_copy(k, m).start()
            return 0

        def own(m, _):
            part = logits_tile(k, c * (HM * MT) + m * MT)
            core_copy(k, m).wait_recv()
            if k < 2:
                ZS[k, m] = (part + PR[k, m].astype(f32)).astype(bf16)
                z_copy(k, m).start()
            else:
                OWN[k - 2, m] = part + PR[k, m].astype(f32)
            return 0

        lax.fori_loop(0, HM, other, 0)
        lax.fori_loop(0, HM, own, 0)

    def one_hot():
        for cp in tok_cps:
            cp.wait_recv()

        def block(n, _):
            i = ((zh + n // 2) % 2) * 2 + (c + n % 2) % 2
            token = jnp.broadcast_to(TOK[i][0:1].astype(f32), (QB, 256)).T
            first = vo * VOC

            def tile(k, _):
                entry = (lax.broadcasted_iota(i32, (256, QB), 1) + (first + k * QB)).astype(f32)
                OH[pl.ds(pl.multiple_of(n * 256, 256), 256), pl.ds(pl.multiple_of(k * QB, QB), QB)] = jnp.where(
                    token == entry, 1.0, 0.0
                ).astype(bf16)
                return 0

            lax.fori_loop(0, VOC // QB, tile, 0)
            return 0

        lax.fori_loop(0, 4, block, 0)

    def pick(lo, hi):
        def tile(n, _):
            cols = pl.ds(pl.multiple_of(n * 256, 256), 256)
            part = jnp.dot(OH[...], EM[:, cols], preferred_element_type=f32)
            PK[:, :, :, :, cols] = part.astype(bf16).reshape(4, 4, 4, 16, 256)
            return 0

        lax.fori_loop(lo, hi, tile, 0)

    LO, HI = pl.ds(0, HALF), pl.ds(HALF, HALF)

    def a_copy(n, j):
        part = pl.ds(0, 2) if j == 0 else pl.ds(2, 2)
        src = PK.at[ys[2], part, :, :, LO] if n == 0 else PK.at[:, part, xs[2], :, HI]
        step = 1 if j == 0 else 3
        target = dev(x, y + step, z, c) if n == 0 else dev(x + step, y, z, c)
        return remote(src, (RA0 if n == 0 else RA1).at[j], a_s.at[n, j], a_r.at[n, j], target)

    def b_copy(n, j):
        step = 1 if j == 0 else 3
        src = PK.at[ys[step], :, :, :, LO] if n == 0 else PK.at[:, :, xs[step], :, HI]
        target = dev(x, y + step, z, c) if n == 0 else dev(x + step, y, z, c)
        return remote(src, RB.at[n, j], b_s.at[n, j], b_r.at[n, j], target)

    def c_copy(n, j):
        src = PK.at[y, :, xs[ring[j]], :, LO] if n == 0 else PK.at[ys[ring[j]], :, x, :, HI]
        target = dev(x + ring[j], y, z, c) if n == 0 else dev(x, y + ring[j], z, c)
        return remote(src, RC.at[n, j], c_s.at[n, j], c_r.at[n, j], target)

    def a_send():
        for n in range(2):
            for j in range(2):
                go(a_copy(n, j))

    def b_send():
        for j in range(2):
            step = 1 if j == 0 else 3
            for n in range(2):
                a_copy(n, j).wait_recv()
                for s in range(2):
                    if n == 0:
                        PK[ys[step], 2 * j + s, :, :, LO] = PK[ys[step], 2 * j + s, :, :, LO] + RA0[j, s]
                    else:
                        PK[:, 2 * j + s, xs[step], :, HI] = PK[:, 2 * j + s, xs[step], :, HI] + RA1[j, :, s]
                go(b_copy(n, j))

    def c_send():
        for n in range(2):
            for j in range(2):
                b_copy(n, j).wait_recv()
            for s in range(4):
                if n == 0:
                    PK[y, s, :, :, LO] = PK[y, s, :, :, LO] + (RB[0, 0, s] + RB[0, 1, s])
                else:
                    PK[:, s, x, :, HI] = PK[:, s, x, :, HI] + (RB[1, 0, :, s] + RB[1, 1, :, s])
            for j in range(3):
                go(c_copy(n, j))

    d_copy = remote(SD, RD, d_s, d_r, dev(x, y, zh * 2 + (1 - zl), c))

    def d_send():
        total = []
        for n in range(2):
            for j in range(3):
                c_copy(n, j).wait_recv()
            cols = LO if n == 0 else HI
            total.append(PK[y, :, x, :, cols] + (RC[n, 0] + RC[n, 1] + RC[n, 2]))
        total = jnp.concatenate(total, axis=2).astype(f32)
        first, second = total[:, :8, :].reshape(32, WID), total[:, 8:, :].reshape(32, WID)
        mine = zl == 0
        SD[...] = jnp.where(mine, second, first).astype(bf16)
        go(d_copy)
        return jnp.where(mine, first, second)

    def d_done(kept):
        d_copy.wait_recv()
        rows = kept + RD[...].astype(f32)
        for s in range(4):
            emb_ref[s] = rows[s * 8 : (s + 1) * 8].astype(bf16)

    def stats(k):
        token = TOK[0][1 + k : 2 + k] + TOK[1][1 + k : 2 + k]

        def tile(m, carry):
            top, total, target = carry
            z_copy(k, m).wait_recv()
            logits = OWN[k, m] + ZR[k, m].astype(f32)
            entry = lax.broadcasted_iota(i32, (MT, 256), 0) + (vo * VOC + c * (HM * MT) + m * MT)
            target = target + jnp.sum(jnp.where(entry == token, logits, 0.0).reshape(MT // 8, 8, 256), axis=0)
            new = jnp.maximum(top, jnp.max(logits.reshape(MT // 8, 8, 256), axis=0))
            part = jnp.sum(jnp.exp(logits.reshape(MT // 8, 8, 256) - new[None]), axis=0)
            return new, total * jnp.exp(top - new) + part, target

        start = (jnp.full((8, 256), -3e38, f32), jnp.zeros((8, 256), f32), jnp.zeros((8, 256), f32))
        top, total, target = lax.fori_loop(0, HM, tile, start)
        new = jnp.max(top, axis=0, keepdims=True)
        total = jnp.sum(total * jnp.exp(top - new), axis=0, keepdims=True)
        return new, total, jnp.sum(target, axis=0, keepdims=True)

    def combine():
        a, b = stats(0), stats(1)
        top, total, target = (jnp.concatenate([p, q], axis=0) for p, q in zip(a, b))
        for stage in range(3):
            ST[stage, 0] = jnp.concatenate([top, total, target, jnp.zeros((2, 256), f32)], axis=0)
            targets = (
                [dev(x, y, z, c + 1), dev(x, y, zh * 2 + 1 - zl, c), dev(x, y, zh * 2 + 1 - zl, c + 1)],
                [dev(x + d, y, z, c) for d in ring],
                [dev(x, y + d, z, c) for d in ring],
            )[stage]
            cps = [
                remote(ST.at[stage, 0], ST.at[stage, 1 + j], st_s.at[stage, j], st_r.at[stage, j], targets[j])
                for j in range(3)
            ]
            for cp in cps:
                go(cp)
            for cp in cps:
                cp.wait_recv()
            got = [ST[stage, j] for j in range(4)]
            tops = [g[0:2] for g in got]
            top = jnp.maximum(jnp.maximum(tops[0], tops[1]), jnp.maximum(tops[2], tops[3]))
            total = sum(g[2:4] * jnp.exp(t - top) for g, t in zip(got, tops))
            target = sum(g[4:6] for g in got)
        logp_ref[...] = jnp.concatenate([target - top - jnp.log(total), jnp.zeros((6, 256), f32)], axis=0)

    restore(0)
    restore(1)
    units()
    p1_send(0)
    p1_send(1)
    restore(2)
    p1_wait(0)
    p2_send(0)
    restore(3)
    p1_wait(1)
    p2_send(1)
    one_hot()
    p3_send(0)
    p1_send(2)
    for cp in e_cps:
        cp.wait()
    pick(0, 1)
    p3_wait(0)
    chunk(0)
    p3_send(1)
    p1_send(3)
    pick(1, 3)
    p3_wait(1)
    chunk(1)
    pick(3, 7)
    a_send()
    p1_wait(2)
    p2_send(2)
    b_send()
    p3_send(2)
    p1_wait(3)
    p2_send(3)
    p3_wait(2)
    chunk(2)
    c_send()
    p3_send(3)
    p3_wait(3)
    chunk(3)
    kept = d_send()
    d_done(kept)
    combine()
    for k in range(4):
        for m in range(HM):
            core_copy(k, m).wait_send()
            if k < 2:
                z_copy(k, m).wait_send()
    for cp in sends:
        cp.wait_send()


def on_device(head_table, embed_table, hidden, norm_gain, tokens):
    core = lax.axis_index("fsdp") % 2
    plain = tokens.reshape(1, 256)
    by_place = tokens.reshape(4, 16, 2, 2).transpose(2, 1, 0, 3).reshape(2, 16, 1, 8)
    mine = lax.broadcasted_iota(i32, (1, 1, 2, 1), 2) == core
    placed = jnp.where(mine, by_place, 0).reshape(2, 256)
    table = jnp.concatenate([plain, placed, jnp.zeros((5, 256), i32)], axis=0)

    dma = pltpu.SemaphoreType.DMA
    pairs = ((8,), (4,), (4, 2, 3), (4, 2, 2), (4, 2, 2), (4, HM), (2, HM), (2, 2), (2, 2), (2, 3), (), (3, 3))
    sems = []
    for shape in pairs:
        sems += [dma(shape) if shape else dma] * 2
    vm, hbm = pl.BlockSpec(memory_space=pltpu.VMEM), pl.BlockSpec(memory_space=pl.ANY)
    logp, emb = pl.pallas_call(
        kernel,
        name="head",
        out_shape=(jax.ShapeDtypeStruct((8, 256), f32), jax.ShapeDtypeStruct((4, 8, WID), bf16)),
        in_specs=[vm, vm, vm, hbm, hbm],
        out_specs=(vm, vm),
        scratch_shapes=[
            pltpu.VMEM((VOC, WID), bf16),
            pltpu.VMEM((VOC, WID), bf16),
            pltpu.VMEM((1024, VOC), bf16),
            pltpu.VMEM((4, 16, HALF), bf16),
            pltpu.VMEM((8, 16, HALF), bf16),
            pltpu.VMEM((4, 8, 256), i32),
            pltpu.VMEM((4, 2, 4, 4, 16, HALF), bf16),
            pltpu.VMEM((4, HM, MT, 256), bf16),
            pltpu.VMEM((4, HM, MT, 256), bf16),
            pltpu.VMEM((2, HM, MT, 256), bf16),
            pltpu.VMEM((2, HM, MT, 256), bf16),
            pltpu.VMEM((2, HM, MT, 256), f32),
            pltpu.VMEM((4, 4, 4, 16, WID), bf16),
            pltpu.VMEM((2, 2, 4, 16, HALF), bf16),
            pltpu.VMEM((2, 4, 2, 16, HALF), bf16),
            pltpu.VMEM((2, 2, 4, 4, 16, HALF), bf16),
            pltpu.VMEM((2, 3, 4, 16, HALF), bf16),
            pltpu.VMEM((32, WID), bf16),
            pltpu.VMEM((32, WID), bf16),
            pltpu.VMEM((3, 4, 8, 256), f32),
            dma((4,)),
            dma((2,)),
            *sems,
        ],
        compiler_params=pltpu.CompilerParams(
            collective_id=0, has_side_effects=True, vmem_limit_bytes=62 * 2**20
        ),
    )(hidden, norm_gain.reshape(1, D), table, head_table, embed_table)
    rows = logp[:2].reshape(2, 16, 2, 4, 2)
    rows = jnp.where(core == 0, rows[:, :, 0], rows[:, :, 1])
    logprobs = rows.transpose(2, 1, 0, 3).reshape(4, 64)
    return (logprobs, emb)


def solution(mesh):
    placed = (
        P("vocab", "fsdp"),
        P("vocab", "fsdp"),
        P(None, ("fsdp", "vocab"), None),
        P(),
        P(None, "fsdp"),
    )
    return jax.shard_map(
        on_device,
        mesh=mesh,
        in_specs=placed,
        out_specs=(P(None, "fsdp"), P(None, "vocab", "fsdp")),
        check_vma=False,
    )
```

```python
import functools

import jax
import jax.numpy as jnp
from jax import lax
from jax.experimental import pallas as pl
from jax.experimental.pallas import tpu as pltpu
from jax.sharding import PartitionSpec as P

MESH = pl.DeviceIdType.MESH
QB = 128
f32, bf16, i32 = jnp.float32, jnp.bfloat16, jnp.int32
VOC = 2560
WID = 1792
HALF = WID // 2
D = 7168
MT = 640
HM = VOC // 2 // MT
ZT = 320
HZ = VOC // 2 // ZT
LOW, HIGH = 1024, 768
DIRECT = (0,)


def remote(src, dst, send_sem, recv_sem, device):
    return pltpu.make_async_remote_copy(
        src_ref=src, dst_ref=dst, send_sem=send_sem, recv_sem=recv_sem, device_id=device, device_id_type=MESH
    )


def kernel(
    h_ref, g_ref, t_ref, w_hbm, e_hbm, logp_ref, emb_ref,
    W, EM, OH, US, UR, TOK, PERM, X, PS, PR, ZS, ZR, OWN, PK, RA0, RA1, RB0, RB1, RC0, RC1, RD, SD, SA, SB,
    w_sem, e_sem, us_s, us_r, tk_s, tk_r, p1_s, p1_r, p2_s, p2_r, p3_s, p3_r,
    co_s, co_r, z_s, z_r, a_s, a_r, b_s, b_r, c_s, c_r, d_s, d_r, sa_s, sa_r, sb_s, sb_r,
):
    fs, vo = lax.axis_index("fsdp"), lax.axis_index("vocab")
    zh, c = fs // 2, fs % 2
    y, x, zl = vo // 8, (vo // 2) % 4, vo % 2
    z = zh * 2 + zl
    zn = zh * 2 + 1 - zl

    def dev(x_, y_, z_, c_):
        x_, y_, z_, c_ = (x_ + 4) % 4, (y_ + 4) % 4, (z_ + 4) % 4, (c_ + 2) % 2
        return ((z_ // 2) * 2 + c_, (y_ * 4 + x_) * 2 + z_ % 2)

    xs = [(x + d) % 4 for d in range(4)]
    ys = [(y + d) % 4 for d in range(4)]
    column = [(i // 2, i % 2) for i in range(8)]
    plane = [(i % 4, i // 4) for i in range(16)]
    ring = (1, 3, 2)
    sends = []

    def go(cp):
        cp.start()
        sends.append(cp)

    w_cps = [
        pltpu.make_async_copy(w_hbm.at[pl.ds(i * 640, 640)], W.at[pl.ds(i * 640, 640)], w_sem.at[i])
        for i in range(4)
    ]
    e_cps = [
        pltpu.make_async_copy(e_hbm.at[pl.ds(i * 1280, 1280)], EM.at[pl.ds(i * 1280, 1280)], e_sem.at[i])
        for i in range(2)
    ]
    for cp in w_cps[:2] + e_cps + w_cps[2:]:
        cp.start()

    barrier = pltpu.get_barrier_semaphore()
    peers = [dev(x, y, z + dz, c + dc) for dz, dc in column[1:]]
    peers += [dev(x + dx, y + dy, z, c) for dx, dy in plane[1:]]
    for peer in peers:
        pl.semaphore_signal(barrier, inc=1, device_id=peer, device_id_type=MESH)

    h = jnp.concatenate([h_ref[s].astype(f32) for s in range(4)], axis=0)
    ms = jnp.sum(h * h, axis=1, keepdims=True) * (1.0 / D)
    normed = h * lax.rsqrt(ms + 1e-06) * g_ref[...]
    for q in range(4):
        lo = normed[:, q * WID : q * WID + HALF]
        hi = normed[:, q * WID + HALF : (q + 1) * WID]
        US[q] = jnp.concatenate([lo, hi], axis=0).astype(bf16)
    UR[0] = US[fs]

    k_ = lax.broadcasted_iota(i32, (256, 512), 0)
    l_ = lax.broadcasted_iota(i32, (256, 512), 1)
    given = ((l_ >> 1) & 3) * 64 + ((l_ >> 4) & 15) * 4 + (l_ >> 8) * 2 + (l_ & 1)
    PERM[...] = jnp.where((k_ == given) & (((l_ >> 3) & 1) == c), 1.0, 0.0).astype(bf16)
    t = t_ref[...].astype(f32)
    plain = jnp.concatenate([t[s : s + 1] for s in range(4)], axis=1)
    top_part = jnp.floor(plain * (1.0 / 16384.0))
    mid_part = jnp.floor((plain - top_part * 16384.0) * (1.0 / 128.0))
    low_part = plain - top_part * 16384.0 - mid_part * 128.0
    parts = jnp.concatenate([top_part, mid_part, low_part, jnp.zeros((5, 256), f32)], axis=0).astype(bf16)
    moved = jnp.dot(parts, PERM[...], preferred_element_type=f32)
    placed = moved[0:1] * 16384.0 + moved[1:2] * 128.0 + moved[2:3]
    TOK[0] = jnp.concatenate([plain, placed[:, :256], placed[:, 256:], jnp.zeros((5, 256), f32)], axis=0)

    pl.semaphore_wait(barrier, len(peers))

    unit_cps = []
    for i, (dz, dc) in enumerate(column):
        z2, c2 = (z + dz) % 4, (c + dc) % 2
        if i:
            unit_cps.append(
                remote(US.at[(z2 // 2) * 2 + c2], UR.at[i], us_s.at[i], us_r.at[i], dev(x, y, z2, c2))
            )
    tok_cps = [
        remote(TOK.at[0], TOK.at[i], tk_s.at[i], tk_r.at[i], dev(x, y, z + 2 * (i // 2), c + i % 2))
        for i in range(1, 4)
    ]
    for cp in unit_cps[:1] + tok_cps + unit_cps[1:]:
        go(cp)

    def restore(part):
        w_cps[part].wait()

        def group(n, _):
            rows = pl.ds(pl.multiple_of(part * 640 + n * QB, QB), QB)
            for j in range(WID // QB):
                block = W[rows, j * QB : (j + 1) * QB].astype(f32)
                scale = (jnp.max(jnp.abs(block), axis=(0, 1), keepdims=True) + 1e-06) / 7.0
                coded = jnp.floor(block / scale + 0.5)
                W[rows, j * QB : (j + 1) * QB] = (coded * scale).astype(bf16)
            return 0

        lax.fori_loop(0, 5, group, 0)

    zs = [z, zn, (z + 2) % 4, (zn + 2) % 4]

    def units(ks):
        for k in ks:
            dz = (z - zs[k] + 4) % 4
            u0 = UR[dz * 2 + c].astype(f32)
            u1 = UR[dz * 2 + (1 - c)].astype(f32)
            X[k, 0, y, x] = jnp.concatenate([u0[:8], u1[:8]], axis=0).astype(bf16)
            X[k, 1, y, x] = jnp.concatenate([u0[8:], u1[8:]], axis=0).astype(bf16)

    def first_unit():
        unit_cps[0].wait_recv()
        units((0,))

    def other_units():
        for cp in unit_cps[1:]:
            cp.wait_recv()
        units((1, 2, 3))

    def p1_copy(k, n, j, px, py):
        slot = X.at[k, n, py, px]
        target = dev(x + ring[j], y, z, c) if n == 0 else dev(x, y + ring[j], z, c)
        return remote(slot, slot, p1_s.at[k, n, j], p1_r.at[k, n, j], target)

    def p1_send(k):
        for j in range(3):
            for n in range(2):
                go(p1_copy(k, n, j, x, y))

    def p1_wait(k):
        for j in range(3):
            p1_copy(k, 0, j, xs[4 - ring[j]], y).wait_recv()
            p1_copy(k, 1, j, x, ys[4 - ring[j]]).wait_recv()

    def p2_copy(k, n, j, at):
        slot = X.at[k, 0, at] if n == 0 else X.at[k, 1, :, at]
        target = dev(x, y + ring[j], z, c) if n == 0 else dev(x + ring[j], y, z, c)
        return remote(slot, slot, p2_s.at[k, n, j], p2_r.at[k, n, j], target)

    def p2_send(k):
        for j in range(3 if k in DIRECT else 2):
            for n in range(2):
                go(p2_copy(k, n, j, y if n == 0 else x))

    def p3_copy(k, n, j, at):
        part = pl.ds(0, 2) if j == 0 else pl.ds(2, 2)
        slot = X.at[k, 0, at, part] if n == 0 else X.at[k, 1, part, at]
        target = dev(x, y + ring[j], z, c) if n == 0 else dev(x + ring[j], y, z, c)
        return remote(slot, slot, p3_s.at[k, n, j], p3_r.at[k, n, j], target)

    def p2_wait(k, n, j):
        came = (ys if n == 0 else xs)[4 - ring[j]]
        p2_copy(k, n, j, came).wait_recv()
        return came

    def p3_send(k):
        for j in range(2):
            for n in range(2):
                go(p3_copy(k, n, j, p2_wait(k, n, j)))

    def gathered(k):
        if k in DIRECT:
            for j in range(3):
                for n in range(2):
                    p2_wait(k, n, j)
        else:
            for j in range(2):
                p3_copy(k, 0, j, ys[2]).wait_recv()
                p3_copy(k, 1, j, xs[2]).wait_recv()

    def logits_tile(k, row):
        rhs = jnp.concatenate([X[k, 0].reshape(256, HALF), X[k, 1].reshape(256, HALF)], axis=1)
        rows = pl.ds(pl.multiple_of(row, MT), MT)
        return lax.dot_general(W[rows, :], rhs, (((1,), (1,)), ((), ())), preferred_element_type=f32)

    def core_copy(k, m):
        return remote(PS.at[k, m], PR.at[k, m], co_s.at[k, m], co_r.at[k, m], dev(x, y, z, c + 1))

    def z_copy(k, m):
        return remote(ZS.at[k, m], ZR.at[k, m], z_s.at[k, m], z_r.at[k, m], dev(x, y, z + 2, c))

    def chunk(k):
        def other(m, _):
            PS[k, m] = logits_tile(k, (1 - c) * (HM * MT) + m * MT).astype(bf16)
            core_copy(k, m).start()
            return 0

        def own(m, _):
            part = logits_tile(k, c * (HM * MT) + m * MT)
            core_copy(k, m).wait_recv()
            both = (part + PR[k, m].astype(f32)).reshape(MT // ZT, ZT, 256)
            here = pl.ds(m * (MT // ZT), MT // ZT)
            if k < 2:
                ZS[k, here] = both.astype(bf16)
                for i in range(MT // ZT):
                    z_copy(k, m * (MT // ZT) + i).start()
            else:
                OWN[k - 2, here] = both
            return 0

        lax.fori_loop(0, HM, other, 0)
        lax.fori_loop(0, HM, own, 0)

    def one_hot():
        for cp in tok_cps:
            cp.wait_recv()

        def block(n, _):
            of = (y + n + 2) % 4
            i = ((zh + of // 2) % 2) * 2 + (c + of % 2) % 2
            token = jnp.broadcast_to(TOK[i][0:1], (QB, 256)).T
            first = vo * VOC

            def tile(k, _):
                entry = (lax.broadcasted_iota(i32, (256, QB), 1) + (first + k * QB)).astype(f32)
                hot = jnp.where(token == entry, 1.0, 0.0).astype(bf16).reshape(4, 4, 16, QB)
                for px in range(4):
                    OH[n, :, (px - x + 6) % 4, :, pl.ds(pl.multiple_of(k * QB, QB), QB)] = hot[:, px]
                return 0

            lax.fori_loop(0, VOC // QB, tile, 0)
            return 0

        lax.fori_loop(0, 4, block, 0)

    def pick(n, first, lo, hi):
        part = pl.ds(0, 1) if first else pl.ds(1, 3)
        slots = 1 if first else 3

        def tile(i, _):
            cols = pl.ds(pl.multiple_of(n * LOW + i * 256, 256), 256)
            hot = OH[part] if n == 0 else OH[:, :, part]
            got = jnp.dot(hot.reshape(slots * 256, VOC), EM[:, cols], preferred_element_type=f32).astype(bf16)
            if n == 0:
                PK[part, :, :, :, cols] = got.reshape(slots, 4, 4, 16, 256)
            else:
                PK[:, :, part, :, cols] = got.reshape(4, 4, slots, 16, 256)
            return 0

        lax.fori_loop(lo, hi, tile, 0)

    LO, HI = pl.ds(0, LOW), pl.ds(LOW, HIGH)

    def along(n, d):
        return dev(x, y + d, z, c) if n == 0 else dev(x + d, y, z, c)

    def a_copy(n, j):
        part = pl.ds(2 * j, 2)
        src = PK.at[0, part, :, :, LO] if n == 0 else PK.at[:, part, 0, :, HI]
        return remote(src, (RA0 if n == 0 else RA1).at[j], a_s.at[n, j], a_r.at[n, j], along(n, ring[j]))

    def b_copy(n, j):
        slot = 3 - 2 * j
        src = PK.at[slot, :, :, :, LO] if n == 0 else PK.at[:, :, slot, :, HI]
        return remote(src, (RB0 if n == 0 else RB1).at[j], b_s.at[n, j], b_r.at[n, j], along(n, ring[j]))

    def c_copy(n, j):
        slot = (ring[j] + 2) % 4
        src = PK.at[2, :, slot, :, LO] if n == 0 else PK.at[slot, :, 2, :, HI]
        return remote(src, (RC0 if n == 0 else RC1).at[j], c_s.at[n, j], c_r.at[n, j], along(1 - n, ring[j]))

    def a_send(n):
        for j in range(2):
            go(a_copy(n, j))

    def b_send(n):
        for j in range(2):
            slot = 3 - 2 * j
            a_copy(n, j).wait_recv()
            for s in range(2):
                if n == 0:
                    PK[slot, 2 * j + s, :, :, LO] = PK[slot, 2 * j + s, :, :, LO] + RA0[j, s]
                else:
                    PK[:, 2 * j + s, slot, :, HI] = PK[:, 2 * j + s, slot, :, HI] + RA1[j, :, s]
            go(b_copy(n, j))

    def c_send(n):
        for j in range(2):
            b_copy(n, j).wait_recv()
        for s in range(4):
            if n == 0:
                PK[2, s, :, :, LO] = PK[2, s, :, :, LO] + (RB0[0, s] + RB0[1, s])
            else:
                PK[:, s, 2, :, HI] = PK[:, s, 2, :, HI] + (RB1[0, :, s] + RB1[1, :, s])
        for j in range(3):
            go(c_copy(n, j))

    d_copy = remote(SD, RD, d_s, d_r, dev(x, y, zn, c))

    def d_send():
        total = []
        for n in range(2):
            for j in range(3):
                c_copy(n, j).wait_recv()
            got = RC0 if n == 0 else RC1
            total.append(PK[2, :, 2, :, LO if n == 0 else HI] + (got[0] + got[1] + got[2]))
        total = jnp.concatenate(total, axis=2).astype(f32)
        first, second = total[:, :8, :].reshape(32, WID), total[:, 8:, :].reshape(32, WID)
        mine = zl == 0
        SD[...] = jnp.where(mine, second, first).astype(bf16)
        go(d_copy)
        return jnp.where(mine, first, second)

    def d_done(kept):
        d_copy.wait_recv()
        rows = kept + RD[...].astype(f32)
        for s in range(4):
            emb_ref[s] = rows[s * 8 : (s + 1) * 8].astype(bf16)

    def stats(k):
        place = zl if k == 0 else 1 - zl
        token = (TOK[2] + TOK[3])[1:3]
        token = jnp.where(place == 0, token[0:1], token[1:2])

        def tile(m, carry):
            top, total, target = carry
            z_copy(k, m).wait_recv()
            logits = (OWN[k, m] + ZR[k, m].astype(f32)).reshape(ZT // 8, 8, 256)
            entry = lax.broadcasted_iota(i32, (ZT, 256), 0) + (vo * VOC + c * (HM * MT) + m * ZT)
            hit = (entry.astype(f32) == token).reshape(ZT // 8, 8, 256)
            target = target + jnp.sum(jnp.where(hit, logits, 0.0), axis=0)
            new = jnp.maximum(top, jnp.max(logits, axis=0))
            part = jnp.sum(jnp.exp(logits - new[None]), axis=0)
            return new, total * jnp.exp(top - new) + part, target

        start = (jnp.full((8, 256), -3e38, f32), jnp.zeros((8, 256), f32), jnp.zeros((8, 256), f32))
        top, total, target = lax.fori_loop(0, HZ, tile, start)
        new = jnp.max(top, axis=0, keepdims=True)
        total = jnp.sum(total * jnp.exp(top - new), axis=0, keepdims=True)
        return new, total, jnp.sum(target, axis=0, keepdims=True)

    def merge(got):
        tops = [g[0:2] for g in got]
        top = functools.reduce(jnp.maximum, tops)
        total = sum(g[2:4] * jnp.exp(t - top) for g, t in zip(got, tops))
        return top, total, sum(g[4:6] for g in got)

    pad = jnp.zeros((2, 256), f32)
    first_targets = [dev(x, y, z_ + 2, c_) for z_ in (z, zn) for c_ in (c, c + 1)]

    def first_copy(j):
        return remote(SA.at[0], SA.at[1 + j], sa_s.at[j], sa_r.at[j], first_targets[j])

    def second_copy(i):
        return remote(SB.at[0], SB.at[i], sb_s.at[i], sb_r.at[i], dev(x + plane[i][0], y + plane[i][1], z, c))

    def first_send(a, b):
        got = [jnp.concatenate(p, axis=0) for p in zip(a, b)]
        got = [jnp.where(zl == 0, g, jnp.concatenate([g[1:2], g[0:1]], axis=0)) for g in got]
        SA[0] = jnp.concatenate([*got, pad], axis=0)
        for j in range(4):
            go(first_copy(j))

    def second_send():
        for j in range(4):
            first_copy(j).wait_recv()
        SB[0] = jnp.concatenate([*merge([SA[1 + j] for j in range(4)]), pad], axis=0)
        for i in range(1, 16):
            go(second_copy(i))

    def finish():
        for i in range(1, 16):
            second_copy(i).wait_recv()
        top, total, target = merge([SB[i] for i in range(16)])
        logp = target - top - jnp.log(total)
        logp = jnp.concatenate([logp[0:1], logp[1:2]], axis=1)
        one = logp.astype(bf16)
        two = (logp - one.astype(f32)).astype(bf16)
        three = (logp - one.astype(f32) - two.astype(f32)).astype(bf16)
        parts = jnp.concatenate(
            [one.astype(f32), two.astype(f32), three.astype(f32), jnp.zeros((5, 512), f32)], axis=0
        ).astype(bf16)
        moved = lax.dot_general(parts, PERM[...], (((1,), (1,)), ((), ())), preferred_element_type=f32)
        row = moved[0:1] + moved[1:2] + moved[2:3]
        logp_ref[...] = jnp.concatenate([row[:, 64 * s : 64 * (s + 1)] for s in range(4)], axis=0)

    restore(0)
    first_unit()
    p1_send(0)
    restore(1)
    one_hot()
    p1_wait(0)
    p2_send(0)
    for cp in e_cps:
        cp.wait()
    pick(0, True, 0, 4)
    a_send(0)
    other_units()
    p1_send(1)
    p1_send(2)
    p1_send(3)
    pick(1, True, 0, 3)
    a_send(1)
    restore(2)
    restore(3)
    p1_wait(1)
    p2_send(1)
    gathered(0)
    chunk(0)
    p1_wait(2)
    p1_wait(3)
    p2_send(2)
    p2_send(3)
    pick(0, False, 0, 4)
    p3_send(1)
    b_send(0)
    pick(1, False, 0, 3)
    b_send(1)
    p3_send(2)
    p3_send(3)
    gathered(1)
    chunk(1)
    c_send(0)
    c_send(1)
    gathered(2)
    chunk(2)
    gathered(3)
    chunk(3)
    early = stats(0)
    kept = d_send()
    first_send(early, stats(1))
    d_done(kept)
    second_send()
    finish()
    for k in range(4):
        for m in range(HM):
            core_copy(k, m).wait_send()
    for k in range(2):
        for m in range(HZ):
            z_copy(k, m).wait_send()
    for cp in sends:
        cp.wait_send()


def hand_over(logp_ref, emb_ref, logp_out, emb_out):
    logp_out[...] = logp_ref[...]
    emb_out[...] = emb_ref[...]


def on_device(head_table, embed_table, hidden, norm_gain, tokens):
    dma = pltpu.SemaphoreType.DMA
    pairs = ((8,), (4,), (4, 2, 3), (4, 2, 3), (4, 2, 2), (4, HM), (2, HZ), (2, 2), (2, 2), (2, 3), (), (4,), (16,))
    sems = []
    for shape in pairs:
        sems += [dma(shape) if shape else dma] * 2
    vm, hbm = pl.BlockSpec(memory_space=pltpu.VMEM), pl.BlockSpec(memory_space=pl.ANY)
    logp, emb = pl.pallas_call(
        kernel,
        name="head",
        out_shape=(jax.ShapeDtypeStruct((4, 64), f32), jax.ShapeDtypeStruct((4, 8, WID), bf16)),
        in_specs=[vm, vm, vm, hbm, hbm],
        out_specs=(vm, vm),
        scratch_shapes=[
            pltpu.VMEM((VOC, WID), bf16),
            pltpu.VMEM((VOC, WID), bf16),
            pltpu.VMEM((4, 4, 4, 16, VOC), bf16),
            pltpu.VMEM((4, 16, HALF), bf16),
            pltpu.VMEM((8, 16, HALF), bf16),
            pltpu.VMEM((4, 8, 256), f32),
            pltpu.VMEM((256, 512), bf16),
            pltpu.VMEM((4, 2, 4, 4, 16, HALF), bf16),
            pltpu.VMEM((4, HM, MT, 256), bf16),
            pltpu.VMEM((4, HM, MT, 256), bf16),
            pltpu.VMEM((2, HZ, ZT, 256), bf16),
            pltpu.VMEM((2, HZ, ZT, 256), bf16),
            pltpu.VMEM((2, HZ, ZT, 256), f32),
            pltpu.VMEM((4, 4, 4, 16, WID), bf16),
            pltpu.VMEM((2, 2, 4, 16, LOW), bf16),
            pltpu.VMEM((2, 4, 2, 16, HIGH), bf16),
            pltpu.VMEM((2, 4, 4, 16, LOW), bf16),
            pltpu.VMEM((2, 4, 4, 16, HIGH), bf16),
            pltpu.VMEM((3, 4, 16, LOW), bf16),
            pltpu.VMEM((3, 4, 16, HIGH), bf16),
            pltpu.VMEM((32, WID), bf16),
            pltpu.VMEM((32, WID), bf16),
            pltpu.VMEM((5, 8, 256), f32),
            pltpu.VMEM((16, 8, 256), f32),
            dma((4,)),
            dma((2,)),
            *sems,
        ],
        compiler_params=pltpu.CompilerParams(
            collective_id=0, has_side_effects=True, vmem_limit_bytes=62 * 2**20
        ),
    )(hidden, norm_gain.reshape(1, D), tokens, head_table, embed_table)
    return pl.pallas_call(
        hand_over,
        name="results",
        out_shape=(jax.ShapeDtypeStruct((4, 64), f32), jax.ShapeDtypeStruct((4, 8, WID), bf16)),
        in_specs=[vm, vm],
        out_specs=(vm, vm),
    )(logp, emb)


def solution(mesh):
    placed = (
        P("vocab", "fsdp"),
        P("vocab", "fsdp"),
        P(None, ("fsdp", "vocab"), None),
        P(),
        P(None, "fsdp"),
    )
    return jax.shard_map(
        on_device,
        mesh=mesh,
        in_specs=placed,
        out_specs=(P(None, "fsdp"), P(None, "vocab", "fsdp")),
        check_vma=False,
    )
```

```python
import functools

import jax
import jax.numpy as jnp
from jax import lax
from jax.experimental import pallas as pl
from jax.experimental.pallas import tpu as pltpu
from jax.sharding import PartitionSpec as P

MESH = pl.DeviceIdType.MESH
QB = 128
f32, bf16, i32 = jnp.float32, jnp.bfloat16, jnp.int32
VOC = 2560
WID = 1792
HALF = WID // 2
D = 7168
MT = 640
HM = VOC // 2 // MT
ZT = 320
HZ = VOC // 2 // ZT
LOW, HIGH = 1024, 768
DIRECT = (0,)


def remote(src, dst, send_sem, recv_sem, device):
    return pltpu.make_async_remote_copy(
        src_ref=src, dst_ref=dst, send_sem=send_sem, recv_sem=recv_sem, device_id=device, device_id_type=MESH
    )


def kernel(
    h_ref, g_ref, t_ref, w_hbm, e_hbm, logp_ref, emb_ref,
    W, EM, OH, US, UR, TOK, PERM, X, PS, PR, ZS, ZR, OWN, PK, RA0, RA1, RB0, RB1, RC0, RC1, RD, SD, SA, SB,
    w_sem, e_sem, us_s, us_r, tk_s, tk_r, p1_s, p1_r, p2_s, p2_r, p3_s, p3_r,
    co_s, co_r, z_s, z_r, a_s, a_r, b_s, b_r, c_s, c_r, d_s, d_r, sa_s, sa_r, sb_s, sb_r,
):
    fs, vo = lax.axis_index("fsdp"), lax.axis_index("vocab")
    zh, c = fs // 2, fs % 2
    y, x, zl = vo // 8, (vo // 2) % 4, vo % 2
    z = zh * 2 + zl
    zn = zh * 2 + 1 - zl

    def dev(x_, y_, z_, c_):
        x_, y_, z_, c_ = (x_ + 4) % 4, (y_ + 4) % 4, (z_ + 4) % 4, (c_ + 2) % 2
        return ((z_ // 2) * 2 + c_, (y_ * 4 + x_) * 2 + z_ % 2)

    xs = [(x + d) % 4 for d in range(4)]
    ys = [(y + d) % 4 for d in range(4)]
    column = [(i // 2, i % 2) for i in range(8)]
    plane = [(i % 4, i // 4) for i in range(16)]
    ring = (1, 3, 2)
    sends = []

    def go(cp):
        cp.start()
        sends.append(cp)

    w_cps = [
        pltpu.make_async_copy(w_hbm.at[pl.ds(i * 640, 640)], W.at[pl.ds(i * 640, 640)], w_sem.at[i])
        for i in range(4)
    ]
    e_cps = [
        pltpu.make_async_copy(e_hbm.at[pl.ds(i * 1280, 1280)], EM.at[pl.ds(i * 1280, 1280)], e_sem.at[i])
        for i in range(2)
    ]
    for cp in w_cps[:2] + e_cps + w_cps[2:]:
        cp.start()

    barrier = pltpu.get_barrier_semaphore()
    peers = [dev(x, y, z + dz, c + dc) for dz, dc in column[1:]]
    peers += [dev(x + dx, y + dy, z, c) for dx, dy in plane[1:]]
    for peer in peers:
        pl.semaphore_signal(barrier, inc=1, device_id=peer, device_id_type=MESH)

    h = jnp.concatenate([h_ref[s].astype(f32) for s in range(4)], axis=0)
    ms = jnp.sum(h * h, axis=1, keepdims=True) * (1.0 / D)
    normed = h * lax.rsqrt(ms + 1e-06) * g_ref[...]
    for q in range(4):
        lo = normed[:, q * WID : q * WID + HALF]
        hi = normed[:, q * WID + HALF : (q + 1) * WID]
        US[q] = jnp.concatenate([lo, hi], axis=0).astype(bf16)
    UR[0] = US[fs]

    k_ = lax.broadcasted_iota(i32, (256, 512), 0)
    l_ = lax.broadcasted_iota(i32, (256, 512), 1)
    given = ((l_ >> 1) & 3) * 64 + ((l_ >> 4) & 15) * 4 + (l_ >> 8) * 2 + (l_ & 1)
    PERM[...] = jnp.where((k_ == given) & (((l_ >> 3) & 1) == c), 1.0, 0.0).astype(bf16)
    t = t_ref[...].astype(f32)
    plain = jnp.concatenate([t[s : s + 1] for s in range(4)], axis=1)
    top_part = jnp.floor(plain * (1.0 / 16384.0))
    mid_part = jnp.floor((plain - top_part * 16384.0) * (1.0 / 128.0))
    low_part = plain - top_part * 16384.0 - mid_part * 128.0
    parts = jnp.concatenate([top_part, mid_part, low_part, jnp.zeros((5, 256), f32)], axis=0).astype(bf16)
    moved = jnp.dot(parts, PERM[...], preferred_element_type=f32)
    placed = moved[0:1] * 16384.0 + moved[1:2] * 128.0 + moved[2:3]
    TOK[0] = jnp.concatenate([plain, placed[:, :256], placed[:, 256:], jnp.zeros((5, 256), f32)], axis=0)

    pl.semaphore_wait(barrier, len(peers))

    unit_cps = []
    for i, (dz, dc) in enumerate(column):
        z2, c2 = (z + dz) % 4, (c + dc) % 2
        if i:
            unit_cps.append(
                remote(US.at[(z2 // 2) * 2 + c2], UR.at[i], us_s.at[i], us_r.at[i], dev(x, y, z2, c2))
            )
    tok_cps = [
        remote(TOK.at[0], TOK.at[i], tk_s.at[i], tk_r.at[i], dev(x, y, z + 2 * (i // 2), c + i % 2))
        for i in range(1, 4)
    ]
    for cp in unit_cps[:1] + tok_cps + unit_cps[1:]:
        go(cp)

    def restore(part):
        w_cps[part].wait()

        def group(n, _):
            rows = pl.ds(pl.multiple_of(part * 640 + n * QB, QB), QB)
            for j in range(WID // QB):
                block = W[rows, j * QB : (j + 1) * QB].astype(f32)
                scale = (jnp.max(jnp.abs(block), axis=(0, 1), keepdims=True) + 1e-06) / 7.0
                coded = jnp.floor(block / scale + 0.5)
                W[rows, j * QB : (j + 1) * QB] = (coded * scale).astype(bf16)
            return 0

        lax.fori_loop(0, 5, group, 0)

    zs = [z, zn, (z + 2) % 4, (zn + 2) % 4]

    def units(ks):
        for k in ks:
            dz = (z - zs[k] + 4) % 4
            u0 = UR[dz * 2 + c].astype(f32)
            u1 = UR[dz * 2 + (1 - c)].astype(f32)
            X[k, 0, y, x] = jnp.concatenate([u0[:8], u1[:8]], axis=0).astype(bf16)
            X[k, 1, y, x] = jnp.concatenate([u0[8:], u1[8:]], axis=0).astype(bf16)

    def first_unit():
        unit_cps[0].wait_recv()
        units((0,))

    def other_units():
        for cp in unit_cps[1:]:
            cp.wait_recv()
        units((1, 2, 3))

    def p1_copy(k, n, j, px, py):
        slot = X.at[k, n, py, px]
        target = dev(x + ring[j], y, z, c) if n == 0 else dev(x, y + ring[j], z, c)
        return remote(slot, slot, p1_s.at[k, n, j], p1_r.at[k, n, j], target)

    def p1_send(k):
        for j in range(3):
            for n in range(2):
                go(p1_copy(k, n, j, x, y))

    def p1_wait(k):
        for j in range(3):
            p1_copy(k, 0, j, xs[4 - ring[j]], y).wait_recv()
            p1_copy(k, 1, j, x, ys[4 - ring[j]]).wait_recv()

    def p2_copy(k, n, j, at):
        slot = X.at[k, 0, at] if n == 0 else X.at[k, 1, :, at]
        target = dev(x, y + ring[j], z, c) if n == 0 else dev(x + ring[j], y, z, c)
        return remote(slot, slot, p2_s.at[k, n, j], p2_r.at[k, n, j], target)

    def p2_send(k):
        for j in range(3 if k in DIRECT else 2):
            for n in range(2):
                go(p2_copy(k, n, j, y if n == 0 else x))

    def p3_copy(k, n, j, at):
        part = pl.ds(0, 2) if j == 0 else pl.ds(2, 2)
        slot = X.at[k, 0, at, part] if n == 0 else X.at[k, 1, part, at]
        target = dev(x, y + ring[j], z, c) if n == 0 else dev(x + ring[j], y, z, c)
        return remote(slot, slot, p3_s.at[k, n, j], p3_r.at[k, n, j], target)

    def p2_wait(k, n, j):
        came = (ys if n == 0 else xs)[4 - ring[j]]
        p2_copy(k, n, j, came).wait_recv()
        return came

    def p3_send(k):
        for j in range(2):
            for n in range(2):
                go(p3_copy(k, n, j, p2_wait(k, n, j)))

    def gathered(k):
        if k in DIRECT:
            for j in range(3):
                for n in range(2):
                    p2_wait(k, n, j)
        else:
            for j in range(2):
                p3_copy(k, 0, j, ys[2]).wait_recv()
                p3_copy(k, 1, j, xs[2]).wait_recv()

    def logits_tile(k, row):
        rhs = jnp.concatenate([X[k, 0].reshape(256, HALF), X[k, 1].reshape(256, HALF)], axis=1)
        rows = pl.ds(pl.multiple_of(row, MT), MT)
        return lax.dot_general(W[rows, :], rhs, (((1,), (1,)), ((), ())), preferred_element_type=f32)

    def core_copy(k, m):
        return remote(PS.at[k, m], PR.at[k, m], co_s.at[k, m], co_r.at[k, m], dev(x, y, z, c + 1))

    def z_copy(k, m):
        return remote(ZS.at[k, m], ZR.at[k, m], z_s.at[k, m], z_r.at[k, m], dev(x, y, z + 2, c))

    def chunk(k):
        def other(m, _):
            PS[k, m] = logits_tile(k, (1 - c) * (HM * MT) + m * MT).astype(bf16)
            core_copy(k, m).start()
            return 0

        def own(m, _):
            part = logits_tile(k, c * (HM * MT) + m * MT)
            core_copy(k, m).wait_recv()
            both = (part + PR[k, m].astype(f32)).reshape(MT // ZT, ZT, 256)
            here = pl.ds(m * (MT // ZT), MT // ZT)
            if k < 2:
                ZS[k, here] = both.astype(bf16)
                for i in range(MT // ZT):
                    z_copy(k, m * (MT // ZT) + i).start()
            else:
                OWN[k - 2, here] = both
            return 0

        lax.fori_loop(0, HM, other, 0)
        lax.fori_loop(0, HM, own, 0)

    def one_hot():
        for cp in tok_cps:
            cp.wait_recv()

        def block(n, _):
            of = (y + ((54 >> (2 * n)) & 3)) % 4
            i = ((zh + of // 2) % 2) * 2 + (c + of % 2) % 2
            token = jnp.broadcast_to(TOK[i][0:1], (QB, 256)).T
            first = vo * VOC

            def tile(k, _):
                entry = (lax.broadcasted_iota(i32, (256, QB), 1) + (first + k * QB)).astype(f32)
                hot = jnp.where(token == entry, 1.0, 0.0).astype(bf16).reshape(4, 4, 16, QB)
                for px in range(4):
                    slot = (135 >> (2 * ((px - x + 4) % 4))) & 3
                    OH[n, :, slot, :, pl.ds(pl.multiple_of(k * QB, QB), QB)] = hot[:, px]
                return 0

            lax.fori_loop(0, VOC // QB, tile, 0)
            return 0

        lax.fori_loop(0, 4, block, 0)

    def pick(n, at, slots):
        part = pl.ds(at, slots)

        def tile(i, _):
            cols = pl.ds(pl.multiple_of(n * LOW + i * 256, 256), 256)
            hot = OH[part] if n == 0 else OH[:, :, part]
            got = jnp.dot(hot.reshape(slots * 256, VOC), EM[:, cols], preferred_element_type=f32).astype(bf16)
            if n == 0:
                PK[part, :, :, :, cols] = got.reshape(slots, 4, 4, 16, 256)
            else:
                PK[:, :, part, :, cols] = got.reshape(4, 4, slots, 16, 256)
            return 0

        lax.fori_loop(0, (HIGH if n else LOW) // 256, tile, 0)

    LO, HI = pl.ds(0, LOW), pl.ds(LOW, HIGH)

    def along(n, d):
        return dev(x, y + d, z, c) if n == 0 else dev(x + d, y, z, c)

    def a_copy(n, j):
        part = pl.ds(2 * j, 2)
        src = PK.at[0, part, :, :, LO] if n == 0 else PK.at[:, part, 0, :, HI]
        return remote(src, (RA0 if n == 0 else RA1).at[j], a_s.at[n, j], a_r.at[n, j], along(n, ring[j]))

    def b_copy(n, j):
        slot = 1 + j
        src = PK.at[slot, :, :, :, LO] if n == 0 else PK.at[:, :, slot, :, HI]
        return remote(src, (RB0 if n == 0 else RB1).at[j], b_s.at[n, j], b_r.at[n, j], along(n, ring[j]))

    def c_copy(n, j):
        slot = (1, 2, 0)[j]
        src = PK.at[3, :, slot, :, LO] if n == 0 else PK.at[slot, :, 3, :, HI]
        return remote(src, (RC0 if n == 0 else RC1).at[j], c_s.at[n, j], c_r.at[n, j], along(1 - n, ring[j]))

    def a_send(n):
        for j in range(2):
            go(a_copy(n, j))

    def b_send(n):
        for j in range(2):
            slot = 1 + j
            a_copy(n, j).wait_recv()
            for s in range(2):
                if n == 0:
                    PK[slot, 2 * j + s, :, :, LO] = PK[slot, 2 * j + s, :, :, LO] + RA0[j, s]
                else:
                    PK[:, 2 * j + s, slot, :, HI] = PK[:, 2 * j + s, slot, :, HI] + RA1[j, :, s]
            go(b_copy(n, j))

    def c_send(n):
        for j in range(2):
            b_copy(n, j).wait_recv()
        for s in range(4):
            if n == 0:
                PK[3, s, :, :, LO] = PK[3, s, :, :, LO] + (RB0[0, s] + RB0[1, s])
            else:
                PK[:, s, 3, :, HI] = PK[:, s, 3, :, HI] + (RB1[0, :, s] + RB1[1, :, s])
        for j in range(3):
            go(c_copy(n, j))

    d_copy = remote(SD, RD, d_s, d_r, dev(x, y, zn, c))

    def d_send():
        total = []
        for n in range(2):
            for j in range(3):
                c_copy(n, j).wait_recv()
            got = RC0 if n == 0 else RC1
            total.append(PK[3, :, 3, :, LO if n == 0 else HI] + (got[0] + got[1] + got[2]))
        total = jnp.concatenate(total, axis=2).astype(f32)
        first, second = total[:, :8, :].reshape(32, WID), total[:, 8:, :].reshape(32, WID)
        mine = zl == 0
        SD[...] = jnp.where(mine, second, first).astype(bf16)
        go(d_copy)
        return jnp.where(mine, first, second)

    def d_done(kept):
        d_copy.wait_recv()
        rows = kept + RD[...].astype(f32)
        for s in range(4):
            emb_ref[s] = rows[s * 8 : (s + 1) * 8].astype(bf16)

    def stats(k):
        place = zl if k == 0 else 1 - zl
        token = (TOK[2] + TOK[3])[1:3]
        token = jnp.where(place == 0, token[0:1], token[1:2])

        def tile(m, carry):
            top, total, target = carry
            z_copy(k, m).wait_recv()
            logits = (OWN[k, m] + ZR[k, m].astype(f32)).reshape(ZT // 8, 8, 256)
            entry = lax.broadcasted_iota(i32, (ZT, 256), 0) + (vo * VOC + c * (HM * MT) + m * ZT)
            hit = (entry.astype(f32) == token).reshape(ZT // 8, 8, 256)
            target = target + jnp.sum(jnp.where(hit, logits, 0.0), axis=0)
            new = jnp.maximum(top, jnp.max(logits, axis=0))
            part = jnp.sum(jnp.exp(logits - new[None]), axis=0)
            return new, total * jnp.exp(top - new) + part, target

        start = (jnp.full((8, 256), -3e38, f32), jnp.zeros((8, 256), f32), jnp.zeros((8, 256), f32))
        top, total, target = lax.fori_loop(0, HZ, tile, start)
        new = jnp.max(top, axis=0, keepdims=True)
        total = jnp.sum(total * jnp.exp(top - new), axis=0, keepdims=True)
        return new, total, jnp.sum(target, axis=0, keepdims=True)

    def merge(got):
        tops = [g[0:2] for g in got]
        top = functools.reduce(jnp.maximum, tops)
        total = sum(g[2:4] * jnp.exp(t - top) for g, t in zip(got, tops))
        return top, total, sum(g[4:6] for g in got)

    pad = jnp.zeros((2, 256), f32)
    first_targets = [dev(x, y, z_ + 2, c_) for z_ in (z, zn) for c_ in (c, c + 1)]

    def first_copy(j):
        return remote(SA.at[0], SA.at[1 + j], sa_s.at[j], sa_r.at[j], first_targets[j])

    def second_copy(i):
        return remote(SB.at[0], SB.at[i], sb_s.at[i], sb_r.at[i], dev(x + plane[i][0], y + plane[i][1], z, c))

    def first_send(a, b):
        got = [jnp.concatenate(p, axis=0) for p in zip(a, b)]
        got = [jnp.where(zl == 0, g, jnp.concatenate([g[1:2], g[0:1]], axis=0)) for g in got]
        SA[0] = jnp.concatenate([*got, pad], axis=0)
        for j in range(4):
            go(first_copy(j))

    def second_send():
        for j in range(4):
            first_copy(j).wait_recv()
        SB[0] = jnp.concatenate([*merge([SA[1 + j] for j in range(4)]), pad], axis=0)
        for i in range(1, 16):
            go(second_copy(i))

    def finish():
        for i in range(1, 16):
            second_copy(i).wait_recv()
        top, total, target = merge([SB[i] for i in range(16)])
        logp = target - top - jnp.log(total)
        logp = jnp.concatenate([logp[0:1], logp[1:2]], axis=1)
        one = logp.astype(bf16)
        two = (logp - one.astype(f32)).astype(bf16)
        three = (logp - one.astype(f32) - two.astype(f32)).astype(bf16)
        parts = jnp.concatenate(
            [one.astype(f32), two.astype(f32), three.astype(f32), jnp.zeros((5, 512), f32)], axis=0
        ).astype(bf16)
        moved = lax.dot_general(parts, PERM[...], (((1,), (1,)), ((), ())), preferred_element_type=f32)
        row = moved[0:1] + moved[1:2] + moved[2:3]
        logp_ref[...] = jnp.concatenate([row[:, 64 * s : 64 * (s + 1)] for s in range(4)], axis=0)

    first_unit()
    p1_send(0)
    restore(0)
    restore(1)
    p1_wait(0)
    p2_send(0)
    one_hot()
    other_units()
    p1_send(1)
    p1_send(2)
    p1_send(3)
    for cp in e_cps:
        cp.wait()
    pick(0, 0, 1)
    a_send(0)
    pick(1, 0, 1)
    p1_wait(1)
    p2_send(1)
    a_send(1)
    restore(2)
    restore(3)
    p1_wait(2)
    p2_send(2)
    p1_wait(3)
    p2_send(3)
    gathered(0)
    chunk(0)
    pick(0, 1, 2)
    p3_send(1)
    b_send(0)
    pick(1, 1, 2)
    b_send(1)
    p3_send(2)
    p3_send(3)
    pick(0, 3, 1)
    pick(1, 3, 1)
    gathered(1)
    chunk(1)
    c_send(0)
    gathered(2)
    chunk(2)
    c_send(1)
    early = stats(0)
    gathered(3)
    chunk(3)
    first_send(early, stats(1))
    kept = d_send()
    second_send()
    d_done(kept)
    finish()
    for k in range(4):
        for m in range(HM):
            core_copy(k, m).wait_send()
    for k in range(2):
        for m in range(HZ):
            z_copy(k, m).wait_send()
    for cp in sends:
        cp.wait_send()


def hand_over(logp_ref, emb_ref, logp_out, emb_out):
    logp_out[...] = logp_ref[...]
    emb_out[...] = emb_ref[...]


def on_device(head_table, embed_table, hidden, norm_gain, tokens):
    dma = pltpu.SemaphoreType.DMA
    pairs = ((8,), (4,), (4, 2, 3), (4, 2, 3), (4, 2, 2), (4, HM), (2, HZ), (2, 2), (2, 2), (2, 3), (), (4,), (16,))
    sems = []
    for shape in pairs:
        sems += [dma(shape) if shape else dma] * 2
    vm, hbm = pl.BlockSpec(memory_space=pltpu.VMEM), pl.BlockSpec(memory_space=pl.ANY)
    logp, emb = pl.pallas_call(
        kernel,
        name="head",
        out_shape=(jax.ShapeDtypeStruct((4, 64), f32), jax.ShapeDtypeStruct((4, 8, WID), bf16)),
        in_specs=[vm, vm, vm, hbm, hbm],
        out_specs=(vm, vm),
        scratch_shapes=[
            pltpu.VMEM((VOC, WID), bf16),
            pltpu.VMEM((VOC, WID), bf16),
            pltpu.VMEM((4, 4, 4, 16, VOC), bf16),
            pltpu.VMEM((4, 16, HALF), bf16),
            pltpu.VMEM((8, 16, HALF), bf16),
            pltpu.VMEM((4, 8, 256), f32),
            pltpu.VMEM((256, 512), bf16),
            pltpu.VMEM((4, 2, 4, 4, 16, HALF), bf16),
            pltpu.VMEM((4, HM, MT, 256), bf16),
            pltpu.VMEM((4, HM, MT, 256), bf16),
            pltpu.VMEM((2, HZ, ZT, 256), bf16),
            pltpu.VMEM((2, HZ, ZT, 256), bf16),
            pltpu.VMEM((2, HZ, ZT, 256), f32),
            pltpu.VMEM((4, 4, 4, 16, WID), bf16),
            pltpu.VMEM((2, 2, 4, 16, LOW), bf16),
            pltpu.VMEM((2, 4, 2, 16, HIGH), bf16),
            pltpu.VMEM((2, 4, 4, 16, LOW), bf16),
            pltpu.VMEM((2, 4, 4, 16, HIGH), bf16),
            pltpu.VMEM((3, 4, 16, LOW), bf16),
            pltpu.VMEM((3, 4, 16, HIGH), bf16),
            pltpu.VMEM((32, WID), bf16),
            pltpu.VMEM((32, WID), bf16),
            pltpu.VMEM((5, 8, 256), f32),
            pltpu.VMEM((16, 8, 256), f32),
            dma((4,)),
            dma((2,)),
            *sems,
        ],
        compiler_params=pltpu.CompilerParams(
            collective_id=0, has_side_effects=True, vmem_limit_bytes=62 * 2**20
        ),
    )(hidden, norm_gain.reshape(1, D), tokens, head_table, embed_table)
    return pl.pallas_call(
        hand_over,
        name="results",
        out_shape=(jax.ShapeDtypeStruct((4, 64), f32), jax.ShapeDtypeStruct((4, 8, WID), bf16)),
        in_specs=[vm, vm],
        out_specs=(vm, vm),
    )(logp, emb)


def solution(mesh):
    placed = (
        P("vocab", "fsdp"),
        P("vocab", "fsdp"),
        P(None, ("fsdp", "vocab"), None),
        P(),
        P(None, "fsdp"),
    )
    return jax.shard_map(
        on_device,
        mesh=mesh,
        in_specs=placed,
        out_specs=(P(None, "fsdp"), P(None, "vocab", "fsdp")),
        check_vma=False,
    )
```

```python
import functools

import jax
import jax.numpy as jnp
from jax import lax
from jax.experimental import pallas as pl
from jax.experimental.pallas import tpu as pltpu
from jax.sharding import PartitionSpec as P

MESH = pl.DeviceIdType.MESH
QB = 128
f32, bf16, i32 = jnp.float32, jnp.bfloat16, jnp.int32
VOC = 2560
WID = 1792
HALF = WID // 2
D = 7168
MT = 640
HM = VOC // 2 // MT
ZT = 320
HZ = VOC // 2 // ZT
LOW, HIGH = 1024, 768
DIRECT = (0,)


def remote(src, dst, send_sem, recv_sem, device):
    return pltpu.make_async_remote_copy(
        src_ref=src, dst_ref=dst, send_sem=send_sem, recv_sem=recv_sem, device_id=device, device_id_type=MESH
    )


def kernel(
    h_hbm, g_hbm, t_hbm, w_hbm, e_hbm, logp_ref, emb_ref,
    h_ref, g_ref, t_ref, W, EM, OH, US, UR, TOK, PERM, X, PS, PR, ZS, ZR, OWN, PK, RA0, RA1, RB0, RB1, RC0, RC1, RD, SD, SA, SB,
    in_sem, w_sem, e_sem, us_s, us_r, tk_s, tk_r, p1_s, p1_r, p2_s, p2_r, p3_s, p3_r,
    co_s, co_r, z_s, z_r, a_s, a_r, b_s, b_r, c_s, c_r, d_s, d_r, sa_s, sa_r, sb_s, sb_r,
):
    fs, vo = lax.axis_index("fsdp"), lax.axis_index("vocab")
    zh, c = fs // 2, fs % 2
    y, x, zl = vo // 8, (vo // 2) % 4, vo % 2
    z = zh * 2 + zl
    zn = zh * 2 + 1 - zl

    def dev(x_, y_, z_, c_):
        x_, y_, z_, c_ = (x_ + 4) % 4, (y_ + 4) % 4, (z_ + 4) % 4, (c_ + 2) % 2
        return ((z_ // 2) * 2 + c_, (y_ * 4 + x_) * 2 + z_ % 2)

    xs = [(x + d) % 4 for d in range(4)]
    ys = [(y + d) % 4 for d in range(4)]
    column = [(i // 2, i % 2) for i in range(8)]
    plane = [(i % 4, i // 4) for i in range(16)]
    ring = (1, 3, 2)
    sends = []

    def go(cp):
        cp.start()
        sends.append(cp)

    barrier = pltpu.get_barrier_semaphore()
    peers = [dev(x, y, z + dz, c + dc) for dz, dc in column[1:]]
    peers += [dev(x + dx, y + dy, z, c) for dx, dy in plane[1:]]
    for peer in peers:
        pl.semaphore_signal(barrier, inc=1, device_id=peer, device_id_type=MESH)

    in_cps = [
        pltpu.make_async_copy(src, dst, in_sem.at[i])
        for i, (src, dst) in enumerate(((h_hbm, h_ref), (g_hbm, g_ref), (t_hbm, t_ref)))
    ]
    for cp in in_cps:
        cp.start()
    for cp in in_cps:
        cp.wait()

    w_cps = [
        pltpu.make_async_copy(w_hbm.at[pl.ds(i * 640, 640)], W.at[pl.ds(i * 640, 640)], w_sem.at[i])
        for i in range(4)
    ]
    e_cps = [
        pltpu.make_async_copy(e_hbm.at[pl.ds(i * 1280, 1280)], EM.at[pl.ds(i * 1280, 1280)], e_sem.at[i])
        for i in range(2)
    ]
    for cp in w_cps[:2] + e_cps + w_cps[2:]:
        cp.start()

    h = jnp.concatenate([h_ref[s].astype(f32) for s in range(4)], axis=0)
    ms = jnp.sum(h * h, axis=1, keepdims=True) * (1.0 / D)
    normed = h * lax.rsqrt(ms + 1e-06) * g_ref[...]
    for q in range(4):
        lo = normed[:, q * WID : q * WID + HALF]
        hi = normed[:, q * WID + HALF : (q + 1) * WID]
        US[q] = jnp.concatenate([lo, hi], axis=0).astype(bf16)
    UR[0] = US[fs]

    k_ = lax.broadcasted_iota(i32, (256, 512), 0)
    l_ = lax.broadcasted_iota(i32, (256, 512), 1)
    given = ((l_ >> 1) & 3) * 64 + ((l_ >> 4) & 15) * 4 + (l_ >> 8) * 2 + (l_ & 1)
    PERM[...] = jnp.where((k_ == given) & (((l_ >> 3) & 1) == c), 1.0, 0.0).astype(bf16)
    t = t_ref[...].astype(f32)
    plain = jnp.concatenate([t[s : s + 1] for s in range(4)], axis=1)
    top_part = jnp.floor(plain * (1.0 / 16384.0))
    mid_part = jnp.floor((plain - top_part * 16384.0) * (1.0 / 128.0))
    low_part = plain - top_part * 16384.0 - mid_part * 128.0
    parts = jnp.concatenate([top_part, mid_part, low_part, jnp.zeros((5, 256), f32)], axis=0).astype(bf16)
    moved = jnp.dot(parts, PERM[...], preferred_element_type=f32)
    placed = moved[0:1] * 16384.0 + moved[1:2] * 128.0 + moved[2:3]
    TOK[0] = jnp.concatenate([plain, placed[:, :256], placed[:, 256:], jnp.zeros((5, 256), f32)], axis=0)

    pl.semaphore_wait(barrier, len(peers))

    unit_cps = []
    for i, (dz, dc) in enumerate(column):
        z2, c2 = (z + dz) % 4, (c + dc) % 2
        if i:
            unit_cps.append(
                remote(US.at[(z2 // 2) * 2 + c2], UR.at[i], us_s.at[i], us_r.at[i], dev(x, y, z2, c2))
            )
    tok_cps = [
        remote(TOK.at[0], TOK.at[i], tk_s.at[i], tk_r.at[i], dev(x, y, z + 2 * (i // 2), c + i % 2))
        for i in range(1, 4)
    ]
    for cp in unit_cps[:1] + tok_cps + unit_cps[1:]:
        go(cp)

    def restore(part):
        w_cps[part].wait()

        def group(n, _):
            rows = pl.ds(pl.multiple_of(part * 640 + n * QB, QB), QB)
            for j in range(WID // QB):
                block = W[rows, j * QB : (j + 1) * QB].astype(f32)
                scale = (jnp.max(jnp.abs(block), axis=(0, 1), keepdims=True) + 1e-06) / 7.0
                coded = jnp.floor(block / scale + 0.5)
                W[rows, j * QB : (j + 1) * QB] = (coded * scale).astype(bf16)
            return 0

        lax.fori_loop(0, 5, group, 0)

    zs = [z, zn, (z + 2) % 4, (zn + 2) % 4]

    def units(ks):
        for k in ks:
            dz = (z - zs[k] + 4) % 4
            u0 = UR[dz * 2 + c].astype(f32)
            u1 = UR[dz * 2 + (1 - c)].astype(f32)
            X[k, 0, y, x] = jnp.concatenate([u0[:8], u1[:8]], axis=0).astype(bf16)
            X[k, 1, y, x] = jnp.concatenate([u0[8:], u1[8:]], axis=0).astype(bf16)

    def first_unit():
        unit_cps[0].wait_recv()
        units((0,))

    def other_units():
        for cp in unit_cps[1:]:
            cp.wait_recv()
        units((1, 2, 3))

    def p1_copy(k, n, j, px, py):
        slot = X.at[k, n, py, px]
        target = dev(x + ring[j], y, z, c) if n == 0 else dev(x, y + ring[j], z, c)
        return remote(slot, slot, p1_s.at[k, n, j], p1_r.at[k, n, j], target)

    def p1_send(k):
        for j in range(3):
            for n in range(2):
                go(p1_copy(k, n, j, x, y))

    def p1_wait(k):
        for j in range(3):
            p1_copy(k, 0, j, xs[4 - ring[j]], y).wait_recv()
            p1_copy(k, 1, j, x, ys[4 - ring[j]]).wait_recv()

    def p2_copy(k, n, j, at):
        slot = X.at[k, 0, at] if n == 0 else X.at[k, 1, :, at]
        target = dev(x, y + ring[j], z, c) if n == 0 else dev(x + ring[j], y, z, c)
        return remote(slot, slot, p2_s.at[k, n, j], p2_r.at[k, n, j], target)

    def p2_send(k):
        for j in range(3 if k in DIRECT else 2):
            for n in range(2):
                go(p2_copy(k, n, j, y if n == 0 else x))

    def p3_copy(k, n, j, at):
        part = pl.ds(0, 2) if j == 0 else pl.ds(2, 2)
        slot = X.at[k, 0, at, part] if n == 0 else X.at[k, 1, part, at]
        target = dev(x, y + ring[j], z, c) if n == 0 else dev(x + ring[j], y, z, c)
        return remote(slot, slot, p3_s.at[k, n, j], p3_r.at[k, n, j], target)

    def p2_wait(k, n, j):
        came = (ys if n == 0 else xs)[4 - ring[j]]
        p2_copy(k, n, j, came).wait_recv()
        return came

    def p3_send(k):
        for j in range(2):
            for n in range(2):
                go(p3_copy(k, n, j, p2_wait(k, n, j)))

    def gathered(k):
        if k in DIRECT:
            for j in range(3):
                for n in range(2):
                    p2_wait(k, n, j)
        else:
            for j in range(2):
                p3_copy(k, 0, j, ys[2]).wait_recv()
                p3_copy(k, 1, j, xs[2]).wait_recv()

    def logits_tile(k, row):
        rhs = jnp.concatenate([X[k, 0].reshape(256, HALF), X[k, 1].reshape(256, HALF)], axis=1)
        rows = pl.ds(pl.multiple_of(row, MT), MT)
        return lax.dot_general(W[rows, :], rhs, (((1,), (1,)), ((), ())), preferred_element_type=f32)

    def core_copy(k, m):
        return remote(PS.at[k, m], PR.at[k, m], co_s.at[k, m], co_r.at[k, m], dev(x, y, z, c + 1))

    def z_copy(k, m):
        return remote(ZS.at[k, m], ZR.at[k, m], z_s.at[k, m], z_r.at[k, m], dev(x, y, z + 2, c))

    def chunk(k):
        def other(m, _):
            PS[k, m] = logits_tile(k, (1 - c) * (HM * MT) + m * MT).astype(bf16)
            core_copy(k, m).start()
            return 0

        def own(m, _):
            part = logits_tile(k, c * (HM * MT) + m * MT)
            core_copy(k, m).wait_recv()
            both = (part + PR[k, m].astype(f32)).reshape(MT // ZT, ZT, 256)
            here = pl.ds(m * (MT // ZT), MT // ZT)
            if k < 2:
                ZS[k, here] = both.astype(bf16)
                for i in range(MT // ZT):
                    z_copy(k, m * (MT // ZT) + i).start()
            else:
                OWN[k - 2, here] = both
            return 0

        lax.fori_loop(0, HM, other, 0)
        lax.fori_loop(0, HM, own, 0)

    def one_hot():
        for cp in tok_cps:
            cp.wait_recv()

        def block(n, _):
            of = (y + ((54 >> (2 * n)) & 3)) % 4
            i = ((zh + of // 2) % 2) * 2 + (c + of % 2) % 2
            token = jnp.broadcast_to(TOK[i][0:1], (QB, 256)).T
            first = vo * VOC

            def tile(k, _):
                entry = (lax.broadcasted_iota(i32, (256, QB), 1) + (first + k * QB)).astype(f32)
                hot = jnp.where(token == entry, 1.0, 0.0).astype(bf16).reshape(4, 4, 16, QB)
                for px in range(4):
                    slot = (135 >> (2 * ((px - x + 4) % 4))) & 3
                    OH[n, :, slot, :, pl.ds(pl.multiple_of(k * QB, QB), QB)] = hot[:, px]
                return 0

            lax.fori_loop(0, VOC // QB, tile, 0)
            return 0

        lax.fori_loop(0, 4, block, 0)

    def pick(n, at, slots):
        part = pl.ds(at, slots)

        def tile(i, _):
            cols = pl.ds(pl.multiple_of(n * LOW + i * 256, 256), 256)
            hot = OH[part] if n == 0 else OH[:, :, part]
            got = jnp.dot(hot.reshape(slots * 256, VOC), EM[:, cols], preferred_element_type=f32).astype(bf16)
            if n == 0:
                PK[part, :, :, :, cols] = got.reshape(slots, 4, 4, 16, 256)
            else:
                PK[:, :, part, :, cols] = got.reshape(4, 4, slots, 16, 256)
            return 0

        lax.fori_loop(0, (HIGH if n else LOW) // 256, tile, 0)

    LO, HI = pl.ds(0, LOW), pl.ds(LOW, HIGH)

    def along(n, d):
        return dev(x, y + d, z, c) if n == 0 else dev(x + d, y, z, c)

    def a_copy(n, j):
        part = pl.ds(2 * j, 2)
        src = PK.at[0, part, :, :, LO] if n == 0 else PK.at[:, part, 0, :, HI]
        return remote(src, (RA0 if n == 0 else RA1).at[j], a_s.at[n, j], a_r.at[n, j], along(n, ring[j]))

    def b_copy(n, j):
        slot = 1 + j
        src = PK.at[slot, :, :, :, LO] if n == 0 else PK.at[:, :, slot, :, HI]
        return remote(src, (RB0 if n == 0 else RB1).at[j], b_s.at[n, j], b_r.at[n, j], along(n, ring[j]))

    def c_copy(n, j):
        slot = (1, 2, 0)[j]
        src = PK.at[3, :, slot, :, LO] if n == 0 else PK.at[slot, :, 3, :, HI]
        return remote(src, (RC0 if n == 0 else RC1).at[j], c_s.at[n, j], c_r.at[n, j], along(1 - n, ring[j]))

    def a_send(n):
        for j in range(2):
            go(a_copy(n, j))

    def b_send(n):
        for j in range(2):
            slot = 1 + j
            a_copy(n, j).wait_recv()
            for s in range(2):
                if n == 0:
                    PK[slot, 2 * j + s, :, :, LO] = PK[slot, 2 * j + s, :, :, LO] + RA0[j, s]
                else:
                    PK[:, 2 * j + s, slot, :, HI] = PK[:, 2 * j + s, slot, :, HI] + RA1[j, :, s]
            go(b_copy(n, j))

    def c_send(n):
        for j in range(2):
            b_copy(n, j).wait_recv()
        for s in range(4):
            if n == 0:
                PK[3, s, :, :, LO] = PK[3, s, :, :, LO] + (RB0[0, s] + RB0[1, s])
            else:
                PK[:, s, 3, :, HI] = PK[:, s, 3, :, HI] + (RB1[0, :, s] + RB1[1, :, s])
        for j in range(3):
            go(c_copy(n, j))

    d_copy = remote(SD, RD, d_s, d_r, dev(x, y, zn, c))

    def d_send():
        total = []
        for n in range(2):
            for j in range(3):
                c_copy(n, j).wait_recv()
            got = RC0 if n == 0 else RC1
            total.append(PK[3, :, 3, :, LO if n == 0 else HI] + (got[0] + got[1] + got[2]))
        total = jnp.concatenate(total, axis=2).astype(f32)
        first, second = total[:, :8, :].reshape(32, WID), total[:, 8:, :].reshape(32, WID)
        mine = zl == 0
        SD[...] = jnp.where(mine, second, first).astype(bf16)
        go(d_copy)
        return jnp.where(mine, first, second)

    def d_done(kept):
        d_copy.wait_recv()
        rows = kept + RD[...].astype(f32)
        for s in range(4):
            emb_ref[s] = rows[s * 8 : (s + 1) * 8].astype(bf16)

    def stats(k):
        place = zl if k == 0 else 1 - zl
        token = (TOK[2] + TOK[3])[1:3]
        token = jnp.where(place == 0, token[0:1], token[1:2])

        def tile(m, carry):
            top, total, target = carry
            z_copy(k, m).wait_recv()
            logits = (OWN[k, m] + ZR[k, m].astype(f32)).reshape(ZT // 8, 8, 256)
            entry = lax.broadcasted_iota(i32, (ZT, 256), 0) + (vo * VOC + c * (HM * MT) + m * ZT)
            hit = (entry.astype(f32) == token).reshape(ZT // 8, 8, 256)
            target = target + jnp.sum(jnp.where(hit, logits, 0.0), axis=0)
            new = jnp.maximum(top, jnp.max(logits, axis=0))
            part = jnp.sum(jnp.exp(logits - new[None]), axis=0)
            return new, total * jnp.exp(top - new) + part, target

        start = (jnp.full((8, 256), -3e38, f32), jnp.zeros((8, 256), f32), jnp.zeros((8, 256), f32))
        top, total, target = lax.fori_loop(0, HZ, tile, start)
        new = jnp.max(top, axis=0, keepdims=True)
        total = jnp.sum(total * jnp.exp(top - new), axis=0, keepdims=True)
        return new, total, jnp.sum(target, axis=0, keepdims=True)

    def merge(got):
        tops = [g[0:2] for g in got]
        top = functools.reduce(jnp.maximum, tops)
        total = sum(g[2:4] * jnp.exp(t - top) for g, t in zip(got, tops))
        return top, total, sum(g[4:6] for g in got)

    pad = jnp.zeros((2, 256), f32)
    first_targets = [dev(x, y, z_ + 2, c_) for z_ in (z, zn) for c_ in (c, c + 1)]

    def first_copy(j):
        return remote(SA.at[0], SA.at[1 + j], sa_s.at[j], sa_r.at[j], first_targets[j])

    def second_copy(i):
        return remote(SB.at[0], SB.at[i], sb_s.at[i], sb_r.at[i], dev(x + plane[i][0], y + plane[i][1], z, c))

    def first_send(a, b):
        got = [jnp.concatenate(p, axis=0) for p in zip(a, b)]
        got = [jnp.where(zl == 0, g, jnp.concatenate([g[1:2], g[0:1]], axis=0)) for g in got]
        SA[0] = jnp.concatenate([*got, pad], axis=0)
        for j in range(4):
            go(first_copy(j))

    def second_send():
        for j in range(4):
            first_copy(j).wait_recv()
        SB[0] = jnp.concatenate([*merge([SA[1 + j] for j in range(4)]), pad], axis=0)
        for i in range(1, 16):
            go(second_copy(i))

    def finish():
        for i in range(1, 16):
            second_copy(i).wait_recv()
        top, total, target = merge([SB[i] for i in range(16)])
        logp = target - top - jnp.log(total)
        logp = jnp.concatenate([logp[0:1], logp[1:2]], axis=1)
        one = logp.astype(bf16)
        two = (logp - one.astype(f32)).astype(bf16)
        three = (logp - one.astype(f32) - two.astype(f32)).astype(bf16)
        parts = jnp.concatenate(
            [one.astype(f32), two.astype(f32), three.astype(f32), jnp.zeros((5, 512), f32)], axis=0
        ).astype(bf16)
        moved = lax.dot_general(parts, PERM[...], (((1,), (1,)), ((), ())), preferred_element_type=f32)
        row = moved[0:1] + moved[1:2] + moved[2:3]
        logp_ref[...] = jnp.concatenate([row[:, 64 * s : 64 * (s + 1)] for s in range(4)], axis=0)

    first_unit()
    p1_send(0)
    restore(0)
    restore(1)
    p1_wait(0)
    p2_send(0)
    one_hot()
    other_units()
    p1_send(1)
    p1_send(2)
    p1_send(3)
    for cp in e_cps:
        cp.wait()
    pick(0, 0, 1)
    a_send(0)
    pick(1, 0, 1)
    p1_wait(1)
    p2_send(1)
    a_send(1)
    restore(2)
    restore(3)
    p1_wait(2)
    p2_send(2)
    p1_wait(3)
    p2_send(3)
    gathered(0)
    chunk(0)
    pick(0, 1, 2)
    p3_send(1)
    b_send(0)
    pick(1, 1, 2)
    b_send(1)
    p3_send(2)
    p3_send(3)
    pick(0, 3, 1)
    pick(1, 3, 1)
    gathered(1)
    chunk(1)
    c_send(0)
    gathered(2)
    chunk(2)
    c_send(1)
    early = stats(0)
    gathered(3)
    chunk(3)
    first_send(early, stats(1))
    kept = d_send()
    second_send()
    d_done(kept)
    finish()
    for k in range(4):
        for m in range(HM):
            core_copy(k, m).wait_send()
    for k in range(2):
        for m in range(HZ):
            z_copy(k, m).wait_send()
    for cp in sends:
        cp.wait_send()


def hand_over(logp_ref, emb_ref, logp_out, emb_out):
    logp_out[...] = logp_ref[...]
    emb_out[...] = emb_ref[...]


def on_device(head_table, embed_table, hidden, norm_gain, tokens):
    dma = pltpu.SemaphoreType.DMA
    pairs = ((8,), (4,), (4, 2, 3), (4, 2, 3), (4, 2, 2), (4, HM), (2, HZ), (2, 2), (2, 2), (2, 3), (), (4,), (16,))
    sems = []
    for shape in pairs:
        sems += [dma(shape) if shape else dma] * 2
    vm, hbm = pl.BlockSpec(memory_space=pltpu.VMEM), pl.BlockSpec(memory_space=pl.ANY)
    logp, emb = pl.pallas_call(
        kernel,
        name="head",
        out_shape=(jax.ShapeDtypeStruct((4, 64), f32), jax.ShapeDtypeStruct((4, 8, WID), bf16)),
        in_specs=[hbm] * 5,
        out_specs=(vm, vm),
        scratch_shapes=[
            pltpu.VMEM((4, 2, D), bf16),
            pltpu.VMEM((1, D), f32),
            pltpu.VMEM((4, 64), i32),
            pltpu.VMEM((VOC, WID), bf16),
            pltpu.VMEM((VOC, WID), bf16),
            pltpu.VMEM((4, 4, 4, 16, VOC), bf16),
            pltpu.VMEM((4, 16, HALF), bf16),
            pltpu.VMEM((8, 16, HALF), bf16),
            pltpu.VMEM((4, 8, 256), f32),
            pltpu.VMEM((256, 512), bf16),
            pltpu.VMEM((4, 2, 4, 4, 16, HALF), bf16),
            pltpu.VMEM((4, HM, MT, 256), bf16),
            pltpu.VMEM((4, HM, MT, 256), bf16),
            pltpu.VMEM((2, HZ, ZT, 256), bf16),
            pltpu.VMEM((2, HZ, ZT, 256), bf16),
            pltpu.VMEM((2, HZ, ZT, 256), f32),
            pltpu.VMEM((4, 4, 4, 16, WID), bf16),
            pltpu.VMEM((2, 2, 4, 16, LOW), bf16),
            pltpu.VMEM((2, 4, 2, 16, HIGH), bf16),
            pltpu.VMEM((2, 4, 4, 16, LOW), bf16),
            pltpu.VMEM((2, 4, 4, 16, HIGH), bf16),
            pltpu.VMEM((3, 4, 16, LOW), bf16),
            pltpu.VMEM((3, 4, 16, HIGH), bf16),
            pltpu.VMEM((32, WID), bf16),
            pltpu.VMEM((32, WID), bf16),
            pltpu.VMEM((5, 8, 256), f32),
            pltpu.VMEM((16, 8, 256), f32),
            dma((3,)),
            dma((4,)),
            dma((2,)),
            *sems,
        ],
        compiler_params=pltpu.CompilerParams(
            collective_id=0, has_side_effects=True, vmem_limit_bytes=62 * 2**20
        ),
    )(hidden, norm_gain.reshape(1, D), tokens, head_table, embed_table)
    return pl.pallas_call(
        hand_over,
        name="results",
        out_shape=(jax.ShapeDtypeStruct((4, 64), f32), jax.ShapeDtypeStruct((4, 8, WID), bf16)),
        in_specs=[vm, vm],
        out_specs=(vm, vm),
    )(logp, emb)


def solution(mesh):
    placed = (
        P("vocab", "fsdp"),
        P("vocab", "fsdp"),
        P(None, ("fsdp", "vocab"), None),
        P(),
        P(None, "fsdp"),
    )
    return jax.shard_map(
        on_device,
        mesh=mesh,
        in_specs=placed,
        out_specs=(P(None, "fsdp"), P(None, "vocab", "fsdp")),
        check_vma=False,
    )
```

```python
import functools

import jax
import jax.numpy as jnp
from jax import lax
from jax.experimental import pallas as pl
from jax.experimental.pallas import tpu as pltpu
from jax.sharding import PartitionSpec as P

MESH = pl.DeviceIdType.MESH
QB = 128
f32, bf16, i32 = jnp.float32, jnp.bfloat16, jnp.int32
VOC = 2560
WID = 1792
HALF = WID // 2
D = 7168
MT = 640
HM = VOC // 2 // MT
ZT = 320
HZ = VOC // 2 // ZT
LOW, HIGH = 1024, 768
DIRECT = (0,)


def remote(src, dst, send_sem, recv_sem, device):
    return pltpu.make_async_remote_copy(
        src_ref=src, dst_ref=dst, send_sem=send_sem, recv_sem=recv_sem, device_id=device, device_id_type=MESH
    )


def kernel(
    h_hbm, g_hbm, t_hbm, w_hbm, e_hbm, logp_ref, emb_ref,
    h_ref, g_ref, t_ref, W, EM, OH, US, UR, TOK, PERM, X, PS, PR, ZS, ZR, OWN, PK, RA0, RA1, RB0, RB1, RC0, RC1, RD, SD, SA, SB,
    in_sem, w_sem, e_sem, us_s, us_r, tk_s, tk_r, p1_s, p1_r, p2_s, p2_r, p3_s, p3_r,
    co_s, co_r, z_s, z_r, a_s, a_r, b_s, b_r, c_s, c_r, d_s, d_r, sa_s, sa_r, sb_s, sb_r,
):
    fs, vo = lax.axis_index("fsdp"), lax.axis_index("vocab")
    zh, c = fs // 2, fs % 2
    y, x, zl = vo // 8, (vo // 2) % 4, vo % 2
    z = zh * 2 + zl
    zn = zh * 2 + 1 - zl

    def dev(x_, y_, z_, c_):
        x_, y_, z_, c_ = (x_ + 4) % 4, (y_ + 4) % 4, (z_ + 4) % 4, (c_ + 2) % 2
        return ((z_ // 2) * 2 + c_, (y_ * 4 + x_) * 2 + z_ % 2)

    xs = [(x + d) % 4 for d in range(4)]
    ys = [(y + d) % 4 for d in range(4)]
    column = [(i // 2, i % 2) for i in range(8)]
    plane = [(i % 4, i // 4) for i in range(16)]
    ring = (1, 3, 2)
    sends = []

    def go(cp):
        cp.start()
        sends.append(cp)

    barrier = pltpu.get_barrier_semaphore()
    peers = [dev(x, y, z + dz, c + dc) for dz, dc in column[1:]]
    peers += [dev(x + dx, y + dy, z, c) for dx, dy in plane[1:]]
    for peer in peers:
        pl.semaphore_signal(barrier, inc=1, device_id=peer, device_id_type=MESH)

    in_cps = [
        pltpu.make_async_copy(src, dst, in_sem.at[i])
        for i, (src, dst) in enumerate(((h_hbm, h_ref), (g_hbm, g_ref), (t_hbm, t_ref)))
    ]
    for cp in in_cps:
        cp.start()
    for cp in in_cps:
        cp.wait()

    w_cps = [
        pltpu.make_async_copy(w_hbm.at[pl.ds(i * 640, 640)], W.at[pl.ds(i * 640, 640)], w_sem.at[i])
        for i in range(4)
    ]
    e_cps = [
        pltpu.make_async_copy(e_hbm.at[pl.ds(i * 1280, 1280)], EM.at[pl.ds(i * 1280, 1280)], e_sem.at[i])
        for i in range(2)
    ]
    for cp in w_cps[:2] + e_cps + w_cps[2:]:
        cp.start()

    h = jnp.concatenate([h_ref[s].astype(f32) for s in range(4)], axis=0)
    ms = jnp.sum(h * h, axis=1, keepdims=True) * (1.0 / D)
    normed = h * lax.rsqrt(ms + 1e-06) * g_ref[...]
    for q in range(4):
        lo = normed[:, q * WID : q * WID + HALF]
        hi = normed[:, q * WID + HALF : (q + 1) * WID]
        US[q] = jnp.concatenate([lo, hi], axis=0).astype(bf16)
    UR[0] = US[fs]

    k_ = lax.broadcasted_iota(i32, (256, 512), 0)
    l_ = lax.broadcasted_iota(i32, (256, 512), 1)
    given = ((l_ >> 1) & 3) * 64 + ((l_ >> 4) & 15) * 4 + (l_ >> 8) * 2 + (l_ & 1)
    PERM[...] = jnp.where((k_ == given) & (((l_ >> 3) & 1) == c), 1.0, 0.0).astype(bf16)
    t = t_ref[...].astype(f32)
    plain = jnp.concatenate([t[s : s + 1] for s in range(4)], axis=1)
    top_part = jnp.floor(plain * (1.0 / 16384.0))
    mid_part = jnp.floor((plain - top_part * 16384.0) * (1.0 / 128.0))
    low_part = plain - top_part * 16384.0 - mid_part * 128.0
    parts = jnp.concatenate([top_part, mid_part, low_part, jnp.zeros((5, 256), f32)], axis=0).astype(bf16)
    moved = jnp.dot(parts, PERM[...], preferred_element_type=f32)
    placed = moved[0:1] * 16384.0 + moved[1:2] * 128.0 + moved[2:3]
    TOK[0] = jnp.concatenate([plain, placed[:, :256], placed[:, 256:], jnp.zeros((5, 256), f32)], axis=0)

    pl.semaphore_wait(barrier, len(peers))

    unit_cps = []
    for i, (dz, dc) in enumerate(column):
        z2, c2 = (z + dz) % 4, (c + dc) % 2
        if i:
            unit_cps.append(
                remote(US.at[(z2 // 2) * 2 + c2], UR.at[i], us_s.at[i], us_r.at[i], dev(x, y, z2, c2))
            )
    tok_cps = [
        remote(TOK.at[0], TOK.at[i], tk_s.at[i], tk_r.at[i], dev(x, y, z + 2 * (i // 2), c + i % 2))
        for i in range(1, 4)
    ]
    for cp in unit_cps[:1] + tok_cps + unit_cps[1:]:
        go(cp)

    def restore(part):
        w_cps[part].wait()

        def group(n, _):
            rows = pl.ds(pl.multiple_of(part * 640 + n * QB, QB), QB)
            for j in range(WID // QB):
                block = W[rows, j * QB : (j + 1) * QB].astype(f32)
                scale = (jnp.max(jnp.abs(block), axis=(0, 1), keepdims=True) + 1e-06) / 7.0
                coded = jnp.floor(block / scale + 0.5)
                W[rows, j * QB : (j + 1) * QB] = (coded * scale).astype(bf16)
            return 0

        lax.fori_loop(0, 5, group, 0)

    zs = [z, zn, (z + 2) % 4, (zn + 2) % 4]

    def units(ks):
        for k in ks:
            dz = (z - zs[k] + 4) % 4
            u0 = UR[dz * 2 + c].astype(f32)
            u1 = UR[dz * 2 + (1 - c)].astype(f32)
            X[k, 0, y, x] = jnp.concatenate([u0[:8], u1[:8]], axis=0).astype(bf16)
            X[k, 1, y, x] = jnp.concatenate([u0[8:], u1[8:]], axis=0).astype(bf16)

    def first_unit():
        unit_cps[0].wait_recv()
        units((0,))

    def other_units():
        for cp in unit_cps[1:]:
            cp.wait_recv()
        units((1, 2, 3))

    def p1_copy(k, n, j, px, py):
        slot = X.at[k, n, py, px]
        target = dev(x + ring[j], y, z, c) if n == 0 else dev(x, y + ring[j], z, c)
        return remote(slot, slot, p1_s.at[k, n, j], p1_r.at[k, n, j], target)

    def p1_send(k):
        for j in range(3):
            for n in range(2):
                go(p1_copy(k, n, j, x, y))

    def p1_wait(k):
        for j in range(3):
            p1_copy(k, 0, j, xs[4 - ring[j]], y).wait_recv()
            p1_copy(k, 1, j, x, ys[4 - ring[j]]).wait_recv()

    def p2_copy(k, n, j, at):
        slot = X.at[k, 0, at] if n == 0 else X.at[k, 1, :, at]
        target = dev(x, y + ring[j], z, c) if n == 0 else dev(x + ring[j], y, z, c)
        return remote(slot, slot, p2_s.at[k, n, j], p2_r.at[k, n, j], target)

    def p2_send(k):
        for j in range(3 if k in DIRECT else 2):
            for n in range(2):
                go(p2_copy(k, n, j, y if n == 0 else x))

    def p3_copy(k, n, j, at):
        part = pl.ds(0, 2) if j == 0 else pl.ds(2, 2)
        slot = X.at[k, 0, at, part] if n == 0 else X.at[k, 1, part, at]
        target = dev(x, y + ring[j], z, c) if n == 0 else dev(x + ring[j], y, z, c)
        return remote(slot, slot, p3_s.at[k, n, j], p3_r.at[k, n, j], target)

    def p2_wait(k, n, j):
        came = (ys if n == 0 else xs)[4 - ring[j]]
        p2_copy(k, n, j, came).wait_recv()
        return came

    def p3_send(k):
        for j in range(2):
            for n in range(2):
                go(p3_copy(k, n, j, p2_wait(k, n, j)))

    def gathered(k):
        if k in DIRECT:
            for j in range(3):
                for n in range(2):
                    p2_wait(k, n, j)
        else:
            for j in range(2):
                p3_copy(k, 0, j, ys[2]).wait_recv()
                p3_copy(k, 1, j, xs[2]).wait_recv()

    def logits_tile(k, row):
        rhs = jnp.concatenate([X[k, 0].reshape(256, HALF), X[k, 1].reshape(256, HALF)], axis=1)
        rows = pl.ds(pl.multiple_of(row, MT), MT)
        return lax.dot_general(W[rows, :], rhs, (((1,), (1,)), ((), ())), preferred_element_type=f32)

    def core_copy(k, m):
        return remote(PS.at[k, m], PR.at[k, m], co_s.at[k, m], co_r.at[k, m], dev(x, y, z, c + 1))

    def z_copy(k, m):
        return remote(ZS.at[k, m], ZR.at[k, m], z_s.at[k, m], z_r.at[k, m], dev(x, y, z + 2, c))

    def chunk(k):
        def other(m, _):
            PS[k, m] = logits_tile(k, (1 - c) * (HM * MT) + m * MT).astype(bf16)
            core_copy(k, m).start()
            return 0

        def own(m, _):
            part = logits_tile(k, c * (HM * MT) + m * MT)
            core_copy(k, m).wait_recv()
            both = (part + PR[k, m].astype(f32)).reshape(MT // ZT, ZT, 256)
            here = pl.ds(m * (MT // ZT), MT // ZT)
            if k < 2:
                ZS[k, here] = both.astype(bf16)
                for i in range(MT // ZT):
                    z_copy(k, m * (MT // ZT) + i).start()
            else:
                OWN[k - 2, here] = both
            return 0

        lax.fori_loop(0, HM, other, 0)
        lax.fori_loop(0, HM, own, 0)

    def one_hot():
        for cp in tok_cps:
            cp.wait_recv()

        def block(n, _):
            of = (y + ((54 >> (2 * n)) & 3)) % 4
            i = ((zh + of // 2) % 2) * 2 + (c + of % 2) % 2
            token = jnp.broadcast_to(TOK[i][0:1], (QB, 256)).T
            first = vo * VOC

            def tile(k, _):
                entry = (lax.broadcasted_iota(i32, (256, QB), 1) + (first + k * QB)).astype(f32)
                hot = jnp.where(token == entry, 1.0, 0.0).astype(bf16).reshape(4, 4, 16, QB)
                for px in range(4):
                    slot = (135 >> (2 * ((px - x + 4) % 4))) & 3
                    OH[n, :, slot, :, pl.ds(pl.multiple_of(k * QB, QB), QB)] = hot[:, px]
                return 0

            lax.fori_loop(0, VOC // QB, tile, 0)
            return 0

        lax.fori_loop(0, 4, block, 0)

    def pick(n, at, slots):
        part = pl.ds(at, slots)

        def tile(i, _):
            cols = pl.ds(pl.multiple_of(n * LOW + i * 256, 256), 256)
            hot = OH[part] if n == 0 else OH[:, :, part]
            got = jnp.dot(hot.reshape(slots * 256, VOC), EM[:, cols], preferred_element_type=f32).astype(bf16)
            if n == 0:
                PK[part, :, :, :, cols] = got.reshape(slots, 4, 4, 16, 256)
            else:
                PK[:, :, part, :, cols] = got.reshape(4, 4, slots, 16, 256)
            return 0

        lax.fori_loop(0, (HIGH if n else LOW) // 256, tile, 0)

    LO, HI = pl.ds(0, LOW), pl.ds(LOW, HIGH)

    def along(n, d):
        return dev(x, y + d, z, c) if n == 0 else dev(x + d, y, z, c)

    def a_copy(n, j):
        part = pl.ds(2 * j, 2)
        src = PK.at[0, part, :, :, LO] if n == 0 else PK.at[:, part, 0, :, HI]
        return remote(src, (RA0 if n == 0 else RA1).at[j], a_s.at[n, j], a_r.at[n, j], along(n, ring[j]))

    def b_copy(n, j):
        slot = 1 + j
        src = PK.at[slot, :, :, :, LO] if n == 0 else PK.at[:, :, slot, :, HI]
        return remote(src, (RB0 if n == 0 else RB1).at[j], b_s.at[n, j], b_r.at[n, j], along(n, ring[j]))

    def c_copy(n, j):
        slot = (1, 2, 0)[j]
        src = PK.at[3, :, slot, :, LO] if n == 0 else PK.at[slot, :, 3, :, HI]
        return remote(src, (RC0 if n == 0 else RC1).at[j], c_s.at[n, j], c_r.at[n, j], along(1 - n, ring[j]))

    def a_send(n):
        for j in range(2):
            go(a_copy(n, j))

    def b_send(n):
        for j in range(2):
            slot = 1 + j
            a_copy(n, j).wait_recv()
            for s in range(2):
                if n == 0:
                    PK[slot, 2 * j + s, :, :, LO] = PK[slot, 2 * j + s, :, :, LO] + RA0[j, s]
                else:
                    PK[:, 2 * j + s, slot, :, HI] = PK[:, 2 * j + s, slot, :, HI] + RA1[j, :, s]
            go(b_copy(n, j))

    def c_send(n):
        for j in range(2):
            b_copy(n, j).wait_recv()
        for s in range(4):
            if n == 0:
                PK[3, s, :, :, LO] = PK[3, s, :, :, LO] + (RB0[0, s] + RB0[1, s])
            else:
                PK[:, s, 3, :, HI] = PK[:, s, 3, :, HI] + (RB1[0, :, s] + RB1[1, :, s])
        for j in range(3):
            go(c_copy(n, j))

    d_copy = remote(SD, RD, d_s, d_r, dev(x, y, zn, c))

    def d_send():
        total = []
        for n in range(2):
            for j in range(3):
                c_copy(n, j).wait_recv()
            got = RC0 if n == 0 else RC1
            total.append(PK[3, :, 3, :, LO if n == 0 else HI] + (got[0] + got[1] + got[2]))
        total = jnp.concatenate(total, axis=2).astype(f32)
        first, second = total[:, :8, :].reshape(32, WID), total[:, 8:, :].reshape(32, WID)
        mine = zl == 0
        SD[...] = jnp.where(mine, second, first).astype(bf16)
        go(d_copy)
        return jnp.where(mine, first, second)

    def d_done(kept):
        d_copy.wait_recv()
        rows = kept + RD[...].astype(f32)
        for s in range(4):
            emb_ref[s] = rows[s * 8 : (s + 1) * 8].astype(bf16)

    def stats(k):
        place = zl if k == 0 else 1 - zl
        token = (TOK[2] + TOK[3])[1:3]
        token = jnp.where(place == 0, token[0:1], token[1:2])

        def tile(m, carry):
            top, total, target = carry
            z_copy(k, m).wait_recv()
            logits = (OWN[k, m] + ZR[k, m].astype(f32)).reshape(ZT // 8, 8, 256)
            entry = lax.broadcasted_iota(i32, (ZT, 256), 0) + (vo * VOC + c * (HM * MT) + m * ZT)
            hit = (entry.astype(f32) == token).reshape(ZT // 8, 8, 256)
            target = target + jnp.sum(jnp.where(hit, logits, 0.0), axis=0)
            new = jnp.maximum(top, jnp.max(logits, axis=0))
            part = jnp.sum(jnp.exp(logits - new[None]), axis=0)
            return new, total * jnp.exp(top - new) + part, target

        start = (jnp.full((8, 256), -3e38, f32), jnp.zeros((8, 256), f32), jnp.zeros((8, 256), f32))
        top, total, target = lax.fori_loop(0, HZ, tile, start)
        new = jnp.max(top, axis=0, keepdims=True)
        total = jnp.sum(total * jnp.exp(top - new), axis=0, keepdims=True)
        return new, total, jnp.sum(target, axis=0, keepdims=True)

    def merge(got):
        tops = [g[0:2] for g in got]
        top = functools.reduce(jnp.maximum, tops)
        total = sum(g[2:4] * jnp.exp(t - top) for g, t in zip(got, tops))
        return top, total, sum(g[4:6] for g in got)

    pad = jnp.zeros((2, 256), f32)
    first_targets = [dev(x, y, z_ + 2, c_) for z_ in (z, zn) for c_ in (c, c + 1)]

    def first_copy(j):
        return remote(SA.at[0], SA.at[1 + j], sa_s.at[j], sa_r.at[j], first_targets[j])

    def second_copy(i):
        return remote(SB.at[0], SB.at[i], sb_s.at[i], sb_r.at[i], dev(x + plane[i][0], y + plane[i][1], z, c))

    def first_send(a, b):
        got = [jnp.concatenate(p, axis=0) for p in zip(a, b)]
        got = [jnp.where(zl == 0, g, jnp.concatenate([g[1:2], g[0:1]], axis=0)) for g in got]
        SA[0] = jnp.concatenate([*got, pad], axis=0)
        for j in range(4):
            go(first_copy(j))

    def second_send():
        for j in range(4):
            first_copy(j).wait_recv()
        SB[0] = jnp.concatenate([*merge([SA[1 + j] for j in range(4)]), pad], axis=0)
        for i in range(1, 16):
            go(second_copy(i))

    def finish():
        for i in range(1, 16):
            second_copy(i).wait_recv()
        top, total, target = merge([SB[i] for i in range(16)])
        logp = target - top - jnp.log(total)
        logp = jnp.concatenate([logp[0:1], logp[1:2]], axis=1)
        one = logp.astype(bf16)
        two = (logp - one.astype(f32)).astype(bf16)
        three = (logp - one.astype(f32) - two.astype(f32)).astype(bf16)
        parts = jnp.concatenate(
            [one.astype(f32), two.astype(f32), three.astype(f32), jnp.zeros((5, 512), f32)], axis=0
        ).astype(bf16)
        moved = lax.dot_general(parts, PERM[...], (((1,), (1,)), ((), ())), preferred_element_type=f32)
        row = moved[0:1] + moved[1:2] + moved[2:3]
        logp_ref[...] = jnp.concatenate([row[:, 64 * s : 64 * (s + 1)] for s in range(4)], axis=0)

    first_unit()
    p1_send(0)
    restore(0)
    restore(1)
    p1_wait(0)
    p2_send(0)
    one_hot()
    other_units()
    p1_send(1)
    p1_send(2)
    p1_send(3)
    for cp in e_cps:
        cp.wait()
    pick(0, 0, 1)
    a_send(0)
    pick(1, 0, 1)
    p1_wait(1)
    p2_send(1)
    a_send(1)
    restore(2)
    restore(3)
    p1_wait(2)
    p2_send(2)
    p1_wait(3)
    p2_send(3)
    gathered(0)
    chunk(0)
    pick(0, 1, 2)
    p3_send(1)
    b_send(0)
    pick(1, 1, 2)
    b_send(1)
    p3_send(2)
    p3_send(3)
    gathered(1)
    chunk(1)
    pick(0, 3, 1)
    pick(1, 3, 1)
    c_send(0)
    gathered(2)
    chunk(2)
    c_send(1)
    early = stats(0)
    gathered(3)
    chunk(3)
    first_send(early, stats(1))
    kept = d_send()
    second_send()
    d_done(kept)
    finish()
    for k in range(4):
        for m in range(HM):
            core_copy(k, m).wait_send()
    for k in range(2):
        for m in range(HZ):
            z_copy(k, m).wait_send()
    for cp in sends:
        cp.wait_send()


def hand_over(logp_ref, emb_ref, logp_out, emb_out, sem):
    cps = [
        pltpu.make_async_copy(emb_ref, emb_out, sem.at[0]),
        pltpu.make_async_copy(logp_ref, logp_out, sem.at[1]),
    ]
    for cp in cps:
        cp.start()
    for cp in cps:
        cp.wait()


def on_device(head_table, embed_table, hidden, norm_gain, tokens):
    dma = pltpu.SemaphoreType.DMA
    pairs = ((8,), (4,), (4, 2, 3), (4, 2, 3), (4, 2, 2), (4, HM), (2, HZ), (2, 2), (2, 2), (2, 3), (), (4,), (16,))
    sems = []
    for shape in pairs:
        sems += [dma(shape) if shape else dma] * 2
    vm, hbm = pl.BlockSpec(memory_space=pltpu.VMEM), pl.BlockSpec(memory_space=pl.ANY)
    logp, emb = pl.pallas_call(
        kernel,
        name="head",
        out_shape=(jax.ShapeDtypeStruct((4, 64), f32), jax.ShapeDtypeStruct((4, 8, WID), bf16)),
        in_specs=[hbm] * 5,
        out_specs=(vm, vm),
        scratch_shapes=[
            pltpu.VMEM((4, 2, D), bf16),
            pltpu.VMEM((1, D), f32),
            pltpu.VMEM((4, 64), i32),
            pltpu.VMEM((VOC, WID), bf16),
            pltpu.VMEM((VOC, WID), bf16),
            pltpu.VMEM((4, 4, 4, 16, VOC), bf16),
            pltpu.VMEM((4, 16, HALF), bf16),
            pltpu.VMEM((8, 16, HALF), bf16),
            pltpu.VMEM((4, 8, 256), f32),
            pltpu.VMEM((256, 512), bf16),
            pltpu.VMEM((4, 2, 4, 4, 16, HALF), bf16),
            pltpu.VMEM((4, HM, MT, 256), bf16),
            pltpu.VMEM((4, HM, MT, 256), bf16),
            pltpu.VMEM((2, HZ, ZT, 256), bf16),
            pltpu.VMEM((2, HZ, ZT, 256), bf16),
            pltpu.VMEM((2, HZ, ZT, 256), f32),
            pltpu.VMEM((4, 4, 4, 16, WID), bf16),
            pltpu.VMEM((2, 2, 4, 16, LOW), bf16),
            pltpu.VMEM((2, 4, 2, 16, HIGH), bf16),
            pltpu.VMEM((2, 4, 4, 16, LOW), bf16),
            pltpu.VMEM((2, 4, 4, 16, HIGH), bf16),
            pltpu.VMEM((3, 4, 16, LOW), bf16),
            pltpu.VMEM((3, 4, 16, HIGH), bf16),
            pltpu.VMEM((32, WID), bf16),
            pltpu.VMEM((32, WID), bf16),
            pltpu.VMEM((5, 8, 256), f32),
            pltpu.VMEM((16, 8, 256), f32),
            dma((3,)),
            dma((4,)),
            dma((2,)),
            *sems,
        ],
        compiler_params=pltpu.CompilerParams(
            collective_id=0, has_side_effects=True, vmem_limit_bytes=62 * 2**20
        ),
    )(hidden, norm_gain.reshape(1, D), tokens, head_table, embed_table)
    return pl.pallas_call(
        hand_over,
        name="results",
        out_shape=(jax.ShapeDtypeStruct((4, 64), f32), jax.ShapeDtypeStruct((4, 8, WID), bf16)),
        in_specs=[hbm, hbm],
        out_specs=(hbm, hbm),
        scratch_shapes=[dma((2,))],
    )(logp, emb)


def solution(mesh):
    placed = (
        P("vocab", "fsdp"),
        P("vocab", "fsdp"),
        P(None, ("fsdp", "vocab"), None),
        P(),
        P(None, "fsdp"),
    )
    return jax.shard_map(
        on_device,
        mesh=mesh,
        in_specs=placed,
        out_specs=(P(None, "fsdp"), P(None, "vocab", "fsdp")),
        check_vma=False,
    )
```
